32 devices in a mesh: section: 2 (over x), dp: 16 (over z, y, core).
Axes of the slice: x: 2, y: 2, z: 4, core: 2. Of those that a mesh axis runs over, the one named last changes fastest.
Arguments:
- section_inputs: bfloat16 [2, 64, 512, 2048], P('section', 'dp'), may hold values from -6 to 6
- neighbours: int32 [64, 512, 16], P('dp'), may hold values from 0 to 511
- counts: int32 [64], P('dp'), may hold values from 102 to 512, as said below
- weight: bfloat16 [2, 2048, 2048], P('section'), may hold values from -0.5 to 0.5
- bias: bfloat16 [2, 2048], P('section'), may hold values from -3 to 3
Outputs:
- activations: bfloat16 [2, 64, 512, 2048], P('section', 'dp')
- boundary_grads: bfloat16 [2, 64, 512, 2048], P('section', 'dp')
- weight_grad: float32 [2, 2048, 2048], P('section')
- bias_grad: float32 [2, 2048], P('section')
The draws below stay inside these ranges and needn't reach their ends.
Inputs may be any that keep to these rules, and one draw needn't show every extreme that they name: `counts`: live nodes of each cluster; slots from the count on are padding.
All inputs are finite; a program needn't handle non-finite values.
Results may differ from the reference program's by a relative error of at most 0.0085.
Values may be sent and summed in bfloat16 or wider, within the bound.
A program may use at most 256 MiB of HBM per device.

```python
import jax
import jax.numpy as jnp
from jax import lax

D = 2048
P_SIZE = 512
K = 16
CLUSTERS = 64


def draw_counts(key, part):
    key = jax.random.fold_in(key, 5)
    first_key, second_key = jax.random.split(key)
    values = jax.random.randint(first_key, (CLUSTERS,), P_SIZE // 5, P_SIZE + 1, dtype=jnp.int32)
    order = jax.random.permutation(second_key, CLUSTERS)
    values = values.at[order[0]].set(P_SIZE)
    values = values.at[order[1]].set(P_SIZE // 5)
    return values.astype(jnp.int32)


def touch_ends(result, key, smallest, largest):
    spot = [jax.random.randint(jax.random.fold_in(key, axis), (), 0, length) for axis, length in enumerate(result.shape)]
    longest = result.shape.index(max(result.shape))
    next_to = spot[:longest] + [(spot[longest] + 1) % result.shape[longest]] + spot[longest + 1:]
    return result.at[tuple(spot)].set(smallest).at[tuple(next_to)].set(largest)


def level_of(rng, shape, cuts, low, high):
    gain, own = 1.0, jax.random.fold_in(rng, 6)
    for axis_at, parts in cuts:
        draws = jnp.exp(jax.random.uniform(jax.random.fold_in(own, axis_at), (parts,), jnp.float32, low / len(cuts), high / len(cuts)))
        gain = gain * jnp.repeat(draws, shape[axis_at] // parts).reshape([-1 if axis == axis_at else 1 for axis in range(len(shape))])
    return gain


def noise(stream_key, dims, width, reach, shards=(), kind=jnp.bfloat16):
    gain = level_of(stream_key, dims, shards, -0.22, 0.18) if shards else 1.0
    values = jax.random.normal(stream_key, dims, jnp.float32) * width * gain
    return jnp.minimum(jnp.maximum(values, -reach), reach).astype(kind)


def setup_inputs(seed: int = 0) -> dict:
    arg_keys = jax.random.split(jax.random.key(seed), 6)
    section_inputs = noise(arg_keys[0], (2, CLUSTERS, P_SIZE, D), 1.0, 6.0, ((0, 2), (1, 16)))
    neighbours = touch_ends(jax.random.randint(arg_keys[1], (CLUSTERS, P_SIZE, K), 0, P_SIZE), jax.random.fold_in(arg_keys[1], 1), 0, P_SIZE - 1).astype(jnp.int32)
    counts = draw_counts(jax.random.fold_in(arg_keys[5], 71), 0)
    weight = noise(arg_keys[3], (2, D, D), (D // 16) ** -0.5, 0.5, ((0, 2),))
    bias = noise(arg_keys[4], (2, D), 0.5, 3.0, ((0, 2),))
    return dict(section_inputs=section_inputs, neighbours=neighbours, counts=counts, weight=weight, bias=bias)


@jax.custom_vjp
def low(v):
    return lax.optimization_barrier(v.astype(jnp.bfloat16)).astype(jnp.float32)

@jax.custom_vjp
def low_back(v):
    return v

def low_keep(v):
    return (low(v), None)

def low_pass(kept, grad):
    return (grad,)

def back_keep(v):
    return (v, None)

def back_low(kept, grad):
    return (low(grad),)
low.defvjp(low_keep, low_pass)
low_back.defvjp(back_keep, back_low)

def normalized(neighbour_rows, live_count, node_slots):
    targets = neighbour_rows % live_count
    columns = jnp.arange(node_slots, dtype=jnp.int32)
    adjacency = lax.optimization_barrier(jnp.sum((targets[:, :, None] == columns[None, None, :]).astype(jnp.float32), axis=1))
    degree = lax.optimization_barrier(jnp.sum(adjacency, axis=1)) + 1.0
    identity = jnp.eye(node_slots, dtype=jnp.float32)
    return (adjacency + adjacency * identity + 2.0 * identity) / degree[:, None]

def layer(inputs, a_hat, live_rows, weight_one, bias_one):
    aggregated = low_back(low(jnp.dot(a_hat, inputs, precision=lax.Precision.HIGHEST, preferred_element_type=jnp.float32)))
    linear_out = low_back(jnp.dot(aggregated, weight_one, precision=lax.Precision.HIGHEST, preferred_element_type=jnp.float32) + bias_one)
    return low(jax.nn.silu(linear_out) * live_rows[:, None])

def reference(section_inputs, neighbours, counts, weight, bias):
    node_slots = section_inputs.shape[2]
    features = section_inputs[0].astype(jnp.float32)
    cotangent = section_inputs[1].astype(jnp.float32)
    weights_all = weight.astype(jnp.float32)
    biases_all = bias.astype(jnp.float32)
    probe_zero = jnp.zeros_like(features)

    def forward(features_in, weight_in, bias_in, probe):

        def cluster(cluster_item):
            rows_in, probe_rows, neighbour_rows, live_count = cluster_item
            a_hat = low(normalized(neighbour_rows, live_count, node_slots))
            live_rows = (jnp.arange(node_slots, dtype=jnp.int32) < live_count).astype(jnp.float32)
            first_out = layer(rows_in, a_hat, live_rows, weight_in[0], bias_in[0])
            hidden = low_back(first_out + probe_rows)
            second_out = layer(hidden, a_hat, live_rows, weight_in[1], bias_in[1])
            return (first_out, second_out)
        return lax.map(jax.checkpoint(cluster), (features_in, probe, neighbours, counts))
    outputs, pullback = jax.vjp(forward, features, weights_all, biases_all, probe_zero)
    grad_in, grad_weight, grad_bias, grad_probe = pullback((jnp.zeros_like(features), cotangent))
    activations = jnp.stack([outputs[0], outputs[1]]).astype(jnp.bfloat16)
    boundary = jnp.stack([grad_in, grad_probe]).astype(jnp.bfloat16)
    return (activations, boundary, grad_weight, grad_bias)
```

```python
import functools

import jax
import jax.numpy as jnp
from jax import lax
from jax.experimental import pallas as pl
from jax.experimental.pallas import tpu as pltpu
from jax.sharding import PartitionSpec as P

MESH = pl.DeviceIdType.MESH
ANY = pl.BlockSpec(memory_space=pl.ANY)
SMEM = pl.BlockSpec(memory_space=pltpu.SMEM)
VMEM = pl.BlockSpec(memory_space=pltpu.VMEM)
F32, BF16 = jnp.float32, jnp.bfloat16

CHUNK = 128
STEP = 128
TILE = 512
COUNT, OFFSET, CHUNKS, LAG = 0, 1, 2, 3


def up(x, by):
    return (x + by - 1) // by * by


def prepare_kernel(
    clusters, slots, packed, counts_ref, targets_ref,
    ahat_ref, plan_ref, agg_ref, dlin_ref, dfac_ref, send_ref, recv_ref, dagg_ref, act_ref, bnd_ref,
    zeros, sem,
):
    c = pl.program_id(0)
    zero_rows = zeros.shape[0]
    total = counts_ref[0] * 0
    for i in range(clusters):
        total = total + up(counts_ref[i], 16)
    chunks = (total + CHUNK - 1) // CHUNK
    start = packed - chunks * CHUNK

    def fills():
        every = recv_ref.shape[0] // zero_rows
        front = (start + CHUNK) // zero_rows
        return [(recv_ref, 0, every), (dagg_ref, 0, every), (agg_ref, 0, front), (dlin_ref, 0, front),
                (dfac_ref, front - 1, front), (send_ref, front - 1, front)]

    def each(act):
        for ref, first, last in fills():
            @pl.loop(first, last)
            def _(i):
                rows = pl.ds(pl.multiple_of(i * zero_rows, zero_rows), zero_rows)
                act(pltpu.make_async_copy(zeros, ref.at[rows], sem))

    @pl.when(c == 0)
    def _():
        zeros[...] = jnp.zeros_like(zeros)
        offset = packed - total
        lag = counts_ref[0] * 0
        for i in range(clusters):
            plan_ref[COUNT, i] = counts_ref[i]
            plan_ref[OFFSET, i] = offset
            first = (offset - start) // CHUNK
            last = (offset + counts_ref[i] - 1 - start) // CHUNK
            lag = jnp.maximum(lag, last - first + 2)
            offset = offset + up(counts_ref[i], 16)
        plan_ref[CHUNKS, 0] = chunks
        plan_ref[LAG, 0] = lag
        each(lambda copy: copy.start())

    count = counts_ref[c]
    slots_each = targets_ref.shape[2]
    group = 64

    @pl.loop(0, slots // group)
    def _(g):
        rows = pl.ds(pl.multiple_of(g * group, group), group)
        targets = targets_ref[0, rows, :]
        columns = lax.broadcasted_iota(jnp.int32, (group, slots), 1)
        row_ids = lax.broadcasted_iota(jnp.int32, (group, slots), 0) + g * group
        adjacency = jnp.zeros((group, slots), F32)
        for k in range(slots_each):
            adjacency = adjacency + jnp.where(targets[:, k:k + 1] == columns, 1.0, 0.0)
        a = jnp.where(row_ids == columns, 2.0 * adjacency + 2.0, adjacency) / (1.0 + slots_each)
        ahat_ref[0, rows, :] = jnp.where(row_ids < count, a, 0.0).astype(BF16)

    @pl.when(c == clusters - 1)
    def _():
        each(lambda copy: copy.wait())


def prepare(counts, targets, width, packed, margin):
    clusters, slots, slots_each = targets.shape
    rows = jax.ShapeDtypeStruct((packed + margin, width), BF16)
    whole = jax.ShapeDtypeStruct((clusters, slots, width), BF16)
    return pl.pallas_call(
        functools.partial(prepare_kernel, clusters, slots, packed),
        grid=(clusters,),
        out_shape=(
            jax.ShapeDtypeStruct((clusters, slots, slots), BF16),
            jax.ShapeDtypeStruct((4, max(clusters, 4)), jnp.int32),
            rows, rows, rows, rows, rows, rows, whole, whole,
        ),
        in_specs=[SMEM, pl.BlockSpec((1, slots, slots_each), lambda c: (c, 0, 0))],
        out_specs=(pl.BlockSpec((1, slots, slots), lambda c: (c, 0, 0)), SMEM) + (ANY,) * 8,
        scratch_shapes=[pltpu.VMEM((CHUNK, width), BF16), pltpu.SemaphoreType.DMA],
        compiler_params=pltpu.CompilerParams(vmem_limit_bytes=40 << 20),
    )(counts, targets)


def tick_kernel(
    clusters, slots, width, packed,
    tick_ref, plan_ref, in_ref, ahat_ref, weight_ref, bias_ref, got_ref,
    agg_i, dlin_i, dfac_i, send_i, recv_i, dagg_i, act_i, bnd_i,
    next_ref, agg_ref, dlin_ref, dfac_ref, send_ref, recv_ref, dagg_ref, act_ref, bnd_ref,
    weight, ahat, rows_in, agg_v, act_v, dfac_v, g_v, d_v, dlin_v, dagg_v, bnd_v, zeros,
    wsem, sem, asem, outsem,
):
    section = lax.axis_index("section")
    tick = tick_ref[0]
    chunks = plan_ref[CHUNKS, 0]
    lag = plan_ref[LAG, 0]
    start = packed - chunks * CHUNK
    is_first = section == 0
    tiles = width // TILE

    def at(i):
        return pl.multiple_of(i, 16)

    def done(copies):
        for copy in copies:
            copy.wait()

    got_chunk = jnp.where(is_first, tick - 1 - lag, tick - 1)
    got_valid = (got_chunk >= 0) & (got_chunk < chunks)
    got_row = start + got_chunk * CHUNK
    fwd_end = jnp.where(is_first, start + (tick + 2) * CHUNK, start + tick * CHUNK)
    bwd_end = got_row + CHUNK

    def fwd_now(c):
        mark = jnp.where(is_first, plan_ref[OFFSET, c], plan_ref[OFFSET, c] + plan_ref[COUNT, c] - 1)
        return (mark >= fwd_end - CHUNK) & (mark < fwd_end)

    def bnd_now(c):
        mark = plan_ref[OFFSET, c] + plan_ref[COUNT, c] - 1
        return (mark >= bwd_end - CHUNK) & (mark < bwd_end)

    any_fwd = fwd_now(0)
    for c in range(1, clusters):
        any_fwd = any_fwd | fwd_now(c)
    any_work = any_fwd | (is_first & got_valid)

    load_weight = pltpu.make_async_copy(weight_ref, weight, wsem)

    @pl.when(any_work)
    def _():
        load_weight.start()

    @pl.when(got_valid & jnp.logical_not(is_first))
    def _():
        copy = pltpu.make_async_copy(got_ref, recv_ref.at[pl.ds(at(got_row), CHUNK)], sem.at[0])
        copy.start()
        copy.wait()

    zeros[...] = jnp.zeros_like(zeros)

    @pl.when(any_work)
    def _():
        load_weight.wait()

    def forward(c):
        offset = plan_ref[OFFSET, c]
        count = plan_ref[COUNT, c]
        steps = (count + STEP - 1) // STEP
        adj = pltpu.make_async_copy(ahat_ref.at[c], ahat, asem)
        adj.start()

        @pl.when(is_first)
        def _():
            pltpu.make_async_copy(in_ref.at[c], rows_in, sem.at[0]).start()

        @pl.when(jnp.logical_not(is_first))
        def _():
            pltpu.make_async_copy(recv_ref.at[pl.ds(at(offset), slots)], rows_in, sem.at[0]).start()

        pltpu.make_async_copy(in_ref.at[c], rows_in, sem.at[0]).wait()
        adj.wait()

        @pl.loop(0, steps)
        def _(r):
            here = pl.ds(pl.multiple_of(r * STEP, STEP), STEP)
            there = pl.ds(at(offset + r * STEP), STEP)
            outs = [
                pltpu.make_async_copy(agg_v, agg_ref.at[there], outsem.at[0]),
                pltpu.make_async_copy(act_v, act_ref.at[c, here], outsem.at[1]),
                pltpu.make_async_copy(dfac_v, dfac_ref.at[there], outsem.at[2]),
            ]
            sent = pltpu.make_async_copy(act_v, send_ref.at[there], outsem.at[3])

            @pl.loop(0, tiles)
            def _(j):
                cols = pl.ds(pl.multiple_of(j * TILE, TILE), TILE)
                agg_v[:, cols] = jnp.dot(ahat[here, :], rows_in[:, cols], preferred_element_type=F32).astype(BF16)

            outs[0].start()
            live = (lax.broadcasted_iota(jnp.int32, (STEP, 1), 0) + r * STEP < count).astype(F32)

            @pl.loop(0, tiles)
            def _(j):
                cols = pl.ds(pl.multiple_of(j * TILE, TILE), TILE)
                linear = jnp.dot(agg_v[...], weight[:, cols], preferred_element_type=F32) + bias_ref[:, cols]
                s = 1.0 / (1.0 + jnp.exp(-linear))
                value = linear * s
                act_v[:, cols] = (value * live).astype(BF16)
                dfac_v[:, cols] = ((s + value * (1.0 - s)) * live).astype(BF16)

            outs[1].start()
            outs[2].start()

            @pl.when(is_first)
            def _():
                sent.start()
                sent.wait()

            done(outs)

        @pl.loop(steps, slots // STEP)
        def _(r):
            copy = pltpu.make_async_copy(zeros, act_ref.at[c, pl.ds(pl.multiple_of(r * STEP, STEP), STEP)], outsem.at[0])
            copy.start()
            copy.wait()

    def backward_rows(row):
        load = pltpu.make_async_copy(dfac_ref.at[pl.ds(at(row), STEP)], d_v, sem.at[1])
        load.start()
        load.wait()
        dlin_v[...] = (g_v[...].astype(F32) * d_v[...].astype(F32)).astype(BF16)
        out = pltpu.make_async_copy(dlin_v, dlin_ref.at[pl.ds(at(row), STEP)], outsem.at[0])
        out.start()

        @pl.loop(0, tiles)
        def _(j):
            cols = pl.ds(pl.multiple_of(j * TILE, TILE), TILE)
            dagg_v[:, cols] = lax.dot_general(
                dlin_v[...], weight[cols, :], (((1,), (1,)), ((), ())), preferred_element_type=F32
            ).astype(BF16)

        out2 = pltpu.make_async_copy(dagg_v, dagg_ref.at[pl.ds(at(row), STEP)], outsem.at[1])
        out2.start()
        done([out, out2])

    def boundary(c):
        offset = plan_ref[OFFSET, c]
        loads = [
            pltpu.make_async_copy(ahat_ref.at[c], ahat, asem),
            pltpu.make_async_copy(dagg_ref.at[pl.ds(at(offset), slots)], rows_in, sem.at[0]),
        ]
        for load in loads:
            load.start()
        done(loads)

        @pl.loop(0, tiles)
        def _(j):
            cols = pl.ds(pl.multiple_of(j * TILE, TILE), TILE)
            bnd_v[:, cols] = lax.dot_general(
                ahat[...], rows_in[:, cols], (((0,), (0,)), ((), ())), preferred_element_type=F32
            ).astype(BF16)

        out = pltpu.make_async_copy(bnd_v, bnd_ref.at[c], outsem.at[0])
        out.start()
        sent = pltpu.make_async_copy(bnd_v, send_ref.at[pl.ds(at(offset), slots)], outsem.at[1])

        @pl.when(jnp.logical_not(is_first))
        def _():
            sent.start()
            sent.wait()

        out.wait()

    @pl.loop(0, clusters)
    def _(c):
        @pl.when(fwd_now(c))
        def _():
            forward(c)

            @pl.when(jnp.logical_not(is_first))
            def _():
                @pl.loop(0, (plan_ref[COUNT, c] + STEP - 1) // STEP)
                def _(r):
                    load = pltpu.make_async_copy(in_ref.at[c, pl.ds(pl.multiple_of(r * STEP, STEP), STEP)], g_v, sem.at[0])
                    load.start()
                    load.wait()
                    backward_rows(plan_ref[OFFSET, c] + r * STEP)

                boundary(c)

    next_chunk = jnp.where(is_first, tick + 1, tick + 1 - lag)

    @pl.when((next_chunk >= 0) & (next_chunk < chunks))
    def _():
        copy = pltpu.make_async_copy(send_ref.at[pl.ds(at(start + next_chunk * CHUNK), CHUNK)], next_ref, sem.at[2])
        copy.start()
        copy.wait()

    @pl.when(is_first & got_valid)
    def _():
        @pl.loop(0, CHUNK // STEP)
        def _(r):
            load = pltpu.make_async_copy(got_ref.at[pl.ds(pl.multiple_of(r * STEP, STEP), STEP)], g_v, sem.at[0])
            load.start()
            load.wait()
            backward_rows(got_row + r * STEP)

        @pl.loop(0, clusters)
        def _(c):
            @pl.when(bnd_now(c))
            def _():
                boundary(c)


def run_tick(tick, plan, section_rows, ahat, weight, bias, got, state, packed):
    clusters, slots, width = section_rows.shape
    state_shapes = tuple(jax.ShapeDtypeStruct(s.shape, s.dtype) for s in state)
    outs = pl.pallas_call(
        functools.partial(tick_kernel, clusters, slots, width, packed),
        out_shape=(jax.ShapeDtypeStruct((CHUNK, width), BF16),) + state_shapes,
        in_specs=[SMEM, SMEM, ANY, ANY, ANY, VMEM, ANY] + [ANY] * 8,
        out_specs=(ANY,) * 9,
        input_output_aliases={7 + i: 1 + i for i in range(8)},
        scratch_shapes=[
            pltpu.VMEM((width, width), BF16),
            pltpu.VMEM((slots, slots), BF16),
            pltpu.VMEM((slots, width), BF16),
            pltpu.VMEM((STEP, width), BF16),
            pltpu.VMEM((STEP, width), BF16),
            pltpu.VMEM((STEP, width), BF16),
            pltpu.VMEM((STEP, width), BF16),
            pltpu.VMEM((STEP, width), BF16),
            pltpu.VMEM((STEP, width), BF16),
            pltpu.VMEM((STEP, width), BF16),
            pltpu.VMEM((slots, width), BF16),
            pltpu.VMEM((STEP, width), BF16),
            pltpu.SemaphoreType.DMA,
            pltpu.SemaphoreType.DMA((3,)),
            pltpu.SemaphoreType.DMA,
            pltpu.SemaphoreType.DMA((4,)),
        ],
        compiler_params=pltpu.CompilerParams(vmem_limit_bytes=40 << 20, has_side_effects=True),
        cost_estimate=pl.CostEstimate(flops=6 * CHUNK * width * width, bytes_accessed=2 * width * width, transcendentals=0),
    )(tick, plan, section_rows, ahat, weight, bias, got, *state)
    return outs[0], outs[1:]


def grads_kernel(n, bits, block, orders, rows, agg_ref, dlin_ref, out_ref, db_ref,
                 lhs, dlin, acc, sbuf, rbuf, res_s, dsend, drecv, dacc,
                 lsem, dsem, ssem, rsem, gssem, grsem, dssem, drsem):
    width = dlin.shape[1]
    nb = len(orders)
    sec = lax.axis_index("section")
    me = lax.axis_index("dp")
    def partner(q):
        bit = (me // 2**q) % 2
        return (sec, me + (1 - 2 * bit) * 2**q)
    barrier = pltpu.get_barrier_semaphore()
    for q in range(bits):
        pl.semaphore_signal(barrier, inc=1, device_id=partner(q), device_id_type=MESH)
    cd = pltpu.make_async_copy(dlin_ref.at[pl.ds(0, rows)], dlin, dsem)
    cd.start()
    def lcopy(b):
        return pltpu.make_async_copy(agg_ref.at[pl.ds(0, rows), pl.ds(b * block, block)], lhs.at[b % 2], lsem.at[b % 2])
    lcopy(0).start()
    cd.wait()
    pl.semaphore_wait(barrier, bits)

    offs = []
    for b in range(nb):
        o = [jnp.int32(0)]
        size = block
        for q in orders[b]:
            size //= 2
            o.append(o[-1] + ((me // 2**q) % 2) * size)
        offs.append(o)
    def rs(b, s):
        q = orders[b][s]
        half = block >> (s + 1)
        base = block - (block >> s)
        return pltpu.make_async_remote_copy(
            src_ref=sbuf.at[b, pl.ds(base, half)], dst_ref=rbuf.at[b, pl.ds(base, half)],
            send_sem=ssem.at[b, s], recv_sem=rsem.at[b, s], device_id=partner(q), device_id_type=MESH)
    def rs_start(b, s):
        q = orders[b][s]
        half = block >> (s + 1)
        base = block - (block >> s)
        bit = (me // 2**q) % 2
        so = pl.multiple_of(offs[b][s] + (1 - bit) * half, 16)
        sbuf[b, pl.ds(base, half), :] = acc[b, pl.ds(so, half), :].astype(jnp.bfloat16)
        rs(b, s).start()
    def rs_end(b, s):
        half = block >> (s + 1)
        base = block - (block >> s)
        rs(b, s).wait_recv()
        ko = pl.multiple_of(offs[b][s + 1], 16)
        acc[b, pl.ds(ko, half), :] += rbuf[b, pl.ds(base, half), :].astype(jnp.float32)
    def ag(b, s):
        q = orders[b][s]
        half = block >> (s + 1)
        o = pl.multiple_of(b * block + offs[b][s + 1], 16)
        return pltpu.make_async_remote_copy(
            src_ref=out_ref.at[pl.ds(o, half)], dst_ref=out_ref.at[pl.ds(o, half)],
            send_sem=gssem.at[b, s], recv_sem=grsem.at[b, s], device_id=partner(q), device_id_type=MESH)
    def ag_recv(b, s):
        q = orders[b][s]
        half = block >> (s + 1)
        bit = (me // 2**q) % 2
        o = pl.multiple_of(b * block + offs[b][s] + (1 - bit) * half, 16)
        return pltpu.make_async_remote_copy(
            src_ref=out_ref.at[pl.ds(o, half)], dst_ref=out_ref.at[pl.ds(o, half)],
            send_sem=gssem.at[b, s], recv_sem=grsem.at[b, s], device_id=partner(q), device_id_type=MESH)
    def matmul(b):
        lcopy(b).wait()
        if b + 1 < nb:
            lcopy(b + 1).start()
        tile, part = 512, min(block, 256)

        @pl.loop(0, block // part)
        def _(i):
            r = pl.ds(pl.multiple_of(i * part, part), part)

            @pl.loop(0, width // tile)
            def _(j):
                c = pl.ds(pl.multiple_of(j * tile, tile), tile)
                acc[b, r, c] = lax.dot_general(lhs[b % 2, :, r], dlin[:, c], (((0,), (0,)), ((), ())), preferred_element_type=jnp.float32)
    def own(b):
        size = block >> bits
        o = pl.multiple_of(offs[b][bits], 16)
        res_s[b] = acc[b, pl.ds(o, size), :].astype(jnp.bfloat16)
        cp = pltpu.make_async_copy(res_s.at[b], out_ref.at[pl.ds(pl.multiple_of(b * block + o, 16), size)], lsem.at[2])
        cp.start()
        cp.wait()
    def stage(b, k):
        if k == 0:
            matmul(b); rs_start(b, 0)
        elif k < bits:
            rs_end(b, k - 1); rs_start(b, k)
        elif k == bits:
            rs_end(b, k - 1); own(b); ag(b, bits - 1).start()
        else:
            s = 2 * bits - k
            ag_recv(b, s).wait_recv()
            if s > 0:
                ag(b, s - 1).start()
    def db_copy(s):
        return pltpu.make_async_remote_copy(src_ref=dsend.at[s], dst_ref=drecv.at[s], send_sem=dssem.at[s], recv_sem=drsem.at[s], device_id=partner(s), device_id_type=MESH)
    dacc[...] = jnp.zeros_like(dacc)
    ones = jnp.ones((16, rows), jnp.bfloat16)
    @pl.loop(0, width // 512)
    def _(j):
        c = pl.ds(pl.multiple_of(j * 512, 512), 512)
        dacc[:, c] = jnp.dot(ones, dlin[:, c], preferred_element_type=jnp.float32)[:8]
    total = 2 * bits + 1
    for step in range(nb + total - 1):
        for k in reversed(range(total)):
            b = step - k
            if 0 <= b < nb:
                stage(b, k)
        if step < bits:
            if step > 0:
                db_copy(step - 1).wait_recv()
                dacc[...] += drecv[step - 1]
            dsend[step] = dacc[...]
            db_copy(step).start()
        elif step == bits:
            db_copy(step - 1).wait_recv()
            dacc[...] += drecv[step - 1]
    db_ref[...] = dacc[...]
    for b in range(nb):
        for s in range(bits):
            rs(b, s).wait_send()
            ag(b, s).wait_send()
    for s in range(bits):
        db_copy(s).wait_send()

def grads(n, agg, dlin, rows, orders=None, collective_id=1):
    width = dlin.shape[1]
    k = agg.shape[1]
    bits = n.bit_length() - 1
    assert 2**bits == n
    block = min(k, max(256, 16 * n))
    nb = k // block
    base = tuple(range(bits))
    if orders is None:
        alt = (0, 2, 1) + base[3:] if bits > 2 else base
        orders = tuple(alt if b % 4 == 2 else base for b in range(nb))
    f = functools.partial(grads_kernel, n, bits, block, orders, rows)
    return pl.pallas_call(
        f,
        out_shape=(jax.ShapeDtypeStruct((k, width), jnp.bfloat16), jax.ShapeDtypeStruct((8, width), jnp.float32)),
        in_specs=[pl.BlockSpec(memory_space=pl.ANY)] * 2,
        out_specs=(pl.BlockSpec(memory_space=pl.ANY), pl.BlockSpec(memory_space=pltpu.VMEM)),
        scratch_shapes=[
            pltpu.VMEM((min(2, nb), rows, block), jnp.bfloat16),
            pltpu.VMEM((rows, width), jnp.bfloat16),
            pltpu.VMEM((nb, block, width), jnp.float32),
            pltpu.VMEM((nb, block, width), jnp.bfloat16),
            pltpu.VMEM((nb, block, width), jnp.bfloat16),
            pltpu.VMEM((nb, block >> bits, width), jnp.bfloat16),
            pltpu.VMEM((bits, 8, width), jnp.float32),
            pltpu.VMEM((bits, 8, width), jnp.float32),
            pltpu.VMEM((8, width), jnp.float32),
            pltpu.SemaphoreType.DMA((3,)),
            pltpu.SemaphoreType.DMA,
            pltpu.SemaphoreType.DMA((nb, bits)),
            pltpu.SemaphoreType.DMA((nb, bits)),
            pltpu.SemaphoreType.DMA((nb, bits)),
            pltpu.SemaphoreType.DMA((nb, bits)),
            pltpu.SemaphoreType.DMA((bits,)),
            pltpu.SemaphoreType.DMA((bits,)),
        ],
        compiler_params=pltpu.CompilerParams(collective_id=collective_id, has_side_effects=True, vmem_limit_bytes=60 << 20),
        cost_estimate=pl.CostEstimate(flops=2 * rows * k * width, bytes_accessed=rows * (k + width) * 2, transcendentals=0),
    )(agg, dlin)


def per_device(section_inputs, neighbours, counts, weight, bias):
    section_rows = section_inputs[0]
    weight_one = weight[0]
    bias_one = bias.astype(F32)
    clusters, slots, width = section_rows.shape
    packed = clusters * slots
    targets = neighbours % counts[:, None, None]
    ahat, plan, *state = prepare(counts, targets, width, packed, slots)
    state = tuple(state)
    swap = [(0, 1), (1, 0)]

    def step(tick, got, state):
        return run_tick(tick, plan, section_rows, ahat, weight_one, bias_one, got, state, packed)

    first = jnp.full((1,), -1, jnp.int32)
    ticks = plan[CHUNKS, 0] + plan[LAG, 0]
    send, state = step(first, section_rows[0, :CHUNK], state)

    def more(carry):
        return carry[0][0] < ticks

    def body(carry):
        tick, send, got, state = carry
        arrives = lax.ppermute(send, "section", swap)
        send, state = step(tick, got, state)
        return tick + 1, send, arrives, state

    tick, send, got, state = lax.while_loop(more, body, (first + 1, send, send, state))
    last, state = step(tick, got, state)
    agg, dlin = state[0], state[1]
    act, bnd = state[6], state[7]
    grad_weight, grad_bias = grads(lax.axis_size("dp"), agg, dlin, packed)
    return act[None], bnd[None], grad_weight.astype(F32)[None], grad_bias[:1]


def solution(mesh):
    return jax.shard_map(
        per_device,
        mesh=mesh,
        in_specs=(
            P("section", "dp", None, None),
            P("dp", None, None),
            P("dp"),
            P("section", None, None),
            P("section", None),
        ),
        out_specs=(
            P("section", "dp", None, None),
            P("section", "dp", None, None),
            P("section", None, None),
            P("section", None),
        ),
        check_vma=False,
    )
```

```python
import functools

import jax
import jax.numpy as jnp
from jax import lax
from jax.experimental import pallas as pl
from jax.experimental.pallas import tpu as pltpu
from jax.sharding import PartitionSpec as P

MESH = pl.DeviceIdType.MESH
ANY = pl.BlockSpec(memory_space=pl.ANY)
SMEM = pl.BlockSpec(memory_space=pltpu.SMEM)
VMEM = pl.BlockSpec(memory_space=pltpu.VMEM)
F32, BF16 = jnp.float32, jnp.bfloat16

CHUNK = 128
STEP = 256
GROUP = 16
TILE = 1024
COUNT, OFFSET, SLOT, REST = 0, 1, 2, 3
CHUNKS = 0


def lag_of(slots):
    return (slots - 1 + CHUNK - 1) // CHUNK + 2


def up(x, by):
    return (x + by - 1) // by * by


def prepare_kernel(
    clusters, slots, packed, counts_ref, neighbours_ref,
    ahat_ref, plan_ref, agg_ref, dlin_ref, dfac_ref, send_ref, recv_ref, dagg_ref, act_ref, bnd_ref,
    zeros, zeros32, sem,
):
    c = pl.program_id(0)
    counts = [counts_ref[i] for i in range(clusters)]
    total = sum(up(n, GROUP) for n in counts)
    chunks = (total + CHUNK - 1) // CHUNK
    start = packed - chunks * CHUNK
    front = (start + CHUNK) // CHUNK
    backlog = packed // CHUNK - lag_of(slots)

    def each(act):
        for ref, first in ((agg_ref, 0), (dlin_ref, 0), (send_ref, jnp.minimum(front - 1, backlog))):
            @pl.loop(first, front)
            def _(i):
                act(pltpu.make_async_copy(zeros, ref.at[pl.ds(pl.multiple_of(i * CHUNK, CHUNK), CHUNK)], sem))

        @pl.loop(backlog, front)
        def _(i):
            act(pltpu.make_async_copy(zeros32, dfac_ref.at[pl.ds(pl.multiple_of(i * CHUNK, CHUNK), CHUNK)], sem))

        for i in range(clusters):
            @pl.loop((counts[i] + GROUP - 1) // GROUP, slots // GROUP)
            def _(g):
                rows = pl.ds(pl.multiple_of(g * GROUP, GROUP), GROUP)
                act(pltpu.make_async_copy(zeros.at[pl.ds(0, GROUP)], act_ref.at[i, rows], sem))

    @pl.when(c == 0)
    def _():
        zeros[...] = jnp.zeros_like(zeros)
        zeros32[...] = jnp.zeros_like(zeros32)
        each(lambda copy: copy.start())
        for i in range(clusters):
            rank = 0
            for j in range(clusters):
                ahead = counts[j] >= counts[i] if j < i else counts[j] > counts[i]
                rank = rank + (ahead.astype(jnp.int32) if j != i else 0)
            plan_ref[COUNT, rank] = counts[i]
            plan_ref[SLOT, rank] = i
        offset = packed - total
        for i in range(clusters):
            plan_ref[OFFSET, i] = offset
            offset = offset + up(plan_ref[COUNT, i], GROUP)
        plan_ref[REST, CHUNKS] = chunks

    count = counts_ref[c]
    slots_each = neighbours_ref.shape[2]
    group = 64

    @pl.loop(0, slots // group)
    def _(g):
        rows = pl.ds(pl.multiple_of(g * group, group), group)
        neighbours = neighbours_ref[0, rows, :]
        times = jnp.floor((neighbours.astype(F32) + 0.5) / count.astype(F32)).astype(jnp.int32)
        targets = neighbours - times * count
        columns = lax.broadcasted_iota(jnp.int32, (group, slots), 1)
        row_ids = lax.broadcasted_iota(jnp.int32, (group, slots), 0) + g * group
        adjacency = jnp.zeros((group, slots), F32)
        for k in range(slots_each):
            adjacency = adjacency + jnp.where(targets[:, k:k + 1] == columns, 1.0, 0.0)
        a = jnp.where(row_ids == columns, 2.0 * adjacency + 2.0, adjacency) / (1.0 + slots_each)
        ahat_ref[0, rows, :] = jnp.where(row_ids < count, a, 0.0).astype(BF16)

    @pl.when(c == clusters - 1)
    def _():
        each(lambda copy: copy.wait())


def prepare(counts, neighbours, width, packed, margin):
    clusters, slots, slots_each = neighbours.shape
    rows = jax.ShapeDtypeStruct((packed + margin, width), BF16)
    rows32 = jax.ShapeDtypeStruct((packed, width), F32)
    whole = jax.ShapeDtypeStruct((clusters, slots, width), BF16)
    return pl.pallas_call(
        functools.partial(prepare_kernel, clusters, slots, packed),
        grid=(clusters,),
        out_shape=(
            jax.ShapeDtypeStruct((clusters, slots, slots), BF16),
            jax.ShapeDtypeStruct((4, max(clusters, 4)), jnp.int32),
            rows, rows, rows32, rows, rows, rows, whole, whole,
        ),
        in_specs=[SMEM, pl.BlockSpec((1, slots, slots_each), lambda c: (c, 0, 0))],
        out_specs=(pl.BlockSpec((1, slots, slots), lambda c: (c, 0, 0)), SMEM) + (ANY,) * 8,
        scratch_shapes=[pltpu.VMEM((CHUNK, width), BF16), pltpu.VMEM((CHUNK, width), F32), pltpu.SemaphoreType.DMA],
        compiler_params=pltpu.CompilerParams(vmem_limit_bytes=40 << 20),
    )(counts, neighbours)


def tick_kernel(
    clusters, slots, width, packed,
    tick_ref, plan_ref, in_ref, ahat_ref, weight_ref, bias_ref, got_ref,
    agg_i, dlin_i, dfac_i, send_i, recv_i, dagg_i, act_i, bnd_i,
    next_ref, agg_ref, dlin_ref, dfac_ref, send_ref, recv_ref, dagg_ref, act_ref, bnd_ref,
    weight, ahat, rows_in, g_v, agg_v, act_v, dlin_v, dagg_v, bnd_v, dfac_v, dback_v,
    wsem, asem, sem, outsem, gsem,
):
    first_section = lax.axis_index("section") == 0
    tick = tick_ref[0]
    chunks = plan_ref[REST, CHUNKS]
    lag = lag_of(slots)
    start = packed - chunks * CHUNK
    tiles = width // TILE
    chunk = pl.ds(0, CHUNK)

    def at(i):
        return pl.multiple_of(i, GROUP)

    def cols(j):
        return pl.ds(j * TILE, TILE)

    def count_of(p):
        return plan_ref[COUNT, p]

    def offset_of(p):
        return plan_ref[OFFSET, p]

    def end_of(p):
        return offset_of(p) + count_of(p)

    load_weight = pltpu.make_async_copy(weight_ref, weight, wsem)

    def load_ahat(p):
        return pltpu.make_async_copy(ahat_ref.at[plan_ref[SLOT, p]], ahat.at[pl.ds(CHUNK, slots)], asem)

    def run(copies):
        for copy in copies:
            copy.start()
        for copy in copies:
            copy.wait()

    def keep_live_rows(ref, count):
        @pl.loop(count // GROUP, slots // GROUP)
        def _(g):
            rows = pl.ds(pl.multiple_of(g * GROUP, GROUP), GROUP)
            live = lax.broadcasted_iota(jnp.int32, (GROUP, 1), 0) + g * GROUP < count
            ref[rows, :] = jnp.where(live, ref[rows, :].astype(F32), 0.0).astype(BF16)

    def silu_of(linear):
        s = 1.0 / (1.0 + jnp.exp(-linear))
        value = linear * s
        return value, s + value * (1.0 - s)

    def boundary(p, source):
        for j in range(tiles):
            bnd_v[:, cols(j)] = lax.dot_general(
                ahat[pl.ds(CHUNK, slots), :], source[:, cols(j)], (((0,), (0,)), ((), ())), preferred_element_type=F32
            ).astype(BF16)

    def first():
        out_chunk = tick + 1
        out_row = start + out_chunk * CHUNK
        out_valid = out_chunk < chunks
        got_chunk = tick - 1 - lag
        got_row = start + got_chunk * CHUNK
        got_valid = (got_chunk >= 0) & (got_chunk < chunks)
        load_g = pltpu.make_async_copy(got_ref.at[chunk], g_v.at[chunk], sem.at[1])
        load_d = pltpu.make_async_copy(dfac_ref.at[pl.ds(at(got_row), CHUNK)], dback_v, sem.at[2])

        @pl.when(out_valid | got_valid)
        def _():
            load_weight.start()

        @pl.when(got_valid)
        def _():
            load_g.start()
            load_d.start()

        @pl.when(out_valid)
        def _():
            zero = jnp.zeros((CHUNK, slots), BF16)
            ahat[pl.ds(0, CHUNK), :] = zero
            ahat[pl.ds(CHUNK + slots, CHUNK), :] = zero
            agg_v[chunk, :] = jnp.zeros((CHUNK, width), BF16)

            @pl.loop(0, clusters)
            def _(p):
                @pl.when((offset_of(p) < out_row + CHUNK) & (end_of(p) > out_row))
                def _():
                    run([load_ahat(p), pltpu.make_async_copy(in_ref.at[plan_ref[SLOT, p]], rows_in, sem.at[0])])
                    a = ahat[pl.ds(at(CHUNK + out_row - offset_of(p)), CHUNK), :]
                    for j in range(tiles):
                        agg_v[chunk, cols(j)] += jnp.dot(a, rows_in[:, cols(j)], preferred_element_type=F32).astype(BF16)

            row_ids = lax.broadcasted_iota(jnp.int32, (CHUNK, 1), 0) + out_row
            live = jnp.zeros((CHUNK, 1), jnp.bool_)
            for p in range(clusters):
                live = live | ((row_ids >= offset_of(p)) & (row_ids < end_of(p)))
            live = live.astype(F32)
            load_weight.wait()
            for j in range(tiles):
                linear = jnp.dot(agg_v[chunk, :], weight[:, cols(j)], preferred_element_type=F32) + bias_ref[:, cols(j)].astype(F32)
                value, factor = silu_of(linear)
                act_v[chunk, cols(j)] = (value * live).astype(BF16)
                dfac_v[:, cols(j)] = factor * live
            there = pl.ds(at(out_row), CHUNK)
            outs = [
                pltpu.make_async_copy(act_v.at[chunk], next_ref, outsem.at[0]),
                pltpu.make_async_copy(agg_v.at[chunk], agg_ref.at[there], outsem.at[1]),
                pltpu.make_async_copy(dfac_v, dfac_ref.at[there], outsem.at[2]),
            ]
            for copy in outs:
                copy.start()

            def groups(act):
                @pl.loop(0, CHUNK // GROUP)
                def _(g):
                    row = out_row + g * GROUP

                    @pl.loop(0, clusters)
                    def _(p):
                        @pl.when((row >= offset_of(p)) & (row < end_of(p)))
                        def _():
                            act(pltpu.make_async_copy(
                                act_v.at[pl.ds(pl.multiple_of(g * GROUP, GROUP), GROUP)],
                                act_ref.at[plan_ref[SLOT, p], pl.ds(at(row - offset_of(p)), GROUP)],
                                gsem,
                            ))

            groups(lambda copy: copy.start())
            groups(lambda copy: copy.wait())
            for copy in outs:
                copy.wait()

        @pl.when(got_valid)
        def _():
            @pl.when(jnp.logical_not(out_valid))
            def _():
                load_weight.wait()

            load_g.wait()
            load_d.wait()
            dlin_v[chunk, :] = (g_v[chunk, :].astype(F32) * dback_v[...]).astype(BF16)
            for j in range(tiles):
                dagg_v[chunk, cols(j)] = lax.dot_general(
                    dlin_v[chunk, :], weight[cols(j), :], (((1,), (1,)), ((), ())), preferred_element_type=F32
                ).astype(BF16)
            there = pl.ds(at(got_row), CHUNK)
            run([
                pltpu.make_async_copy(dlin_v.at[chunk], dlin_ref.at[there], outsem.at[0]),
                pltpu.make_async_copy(dagg_v.at[chunk], dagg_ref.at[there], outsem.at[1]),
            ])

            @pl.loop(0, clusters)
            def _(p):
                last = end_of(p) - 1

                @pl.when((last >= got_row) & (last < got_row + CHUNK))
                def _():
                    run([load_ahat(p), pltpu.make_async_copy(dagg_ref.at[pl.ds(at(offset_of(p)), slots)], rows_in, sem.at[0])])
                    keep_live_rows(rows_in, count_of(p))
                    boundary(p, rows_in)
                    run([pltpu.make_async_copy(bnd_v, bnd_ref.at[plan_ref[SLOT, p]], outsem.at[0])])

    def second():
        got_chunk = tick - 1
        got_row = start + got_chunk * CHUNK
        got_valid = (got_chunk >= 0) & (got_chunk < chunks)

        def complete(p):
            last = end_of(p) - 1
            return got_valid & (last >= got_row) & (last < got_row + CHUNK)

        any_complete = complete(0)
        first_done = jnp.where(any_complete, 0, clusters)
        for p in range(1, clusters):
            first_done = jnp.where(complete(p) & jnp.logical_not(any_complete), p, first_done)
            any_complete = any_complete | complete(p)

        @pl.when(any_complete)
        def _():
            load_weight.start()

        @pl.when(got_valid)
        def _():
            run([pltpu.make_async_copy(got_ref.at[chunk], recv_ref.at[pl.ds(at(got_row), CHUNK)], sem.at[0])])

        @pl.loop(0, clusters)
        def _(p):
            @pl.when(complete(p))
            def _():
                offset, count, slot = offset_of(p), count_of(p), plan_ref[SLOT, p]
                load_g = pltpu.make_async_copy(in_ref.at[slot], g_v, sem.at[1])
                load_g.start()
                run([load_ahat(p), pltpu.make_async_copy(recv_ref.at[pl.ds(at(offset), slots)], rows_in, sem.at[0])])
                keep_live_rows(rows_in, count)
                for j in range(tiles):
                    agg_v[:, cols(j)] = jnp.dot(ahat[pl.ds(CHUNK, slots), :], rows_in[:, cols(j)], preferred_element_type=F32).astype(BF16)
                load_g.wait()

                @pl.when(p == first_done)
                def _():
                    load_weight.wait()

                steps = (count + STEP - 1) // STEP

                def outs(r):
                    here = pl.ds(pl.multiple_of(r * STEP, STEP), STEP)
                    there = pl.ds(at(offset + r * STEP), STEP)
                    return [
                        pltpu.make_async_copy(agg_v.at[here], agg_ref.at[there], outsem.at[0]),
                        pltpu.make_async_copy(act_v.at[here], act_ref.at[slot, here], outsem.at[1]),
                        pltpu.make_async_copy(dlin_v.at[here], dlin_ref.at[there], outsem.at[2]),
                    ]

                @pl.loop(0, steps)
                def _(r):
                    here = pl.ds(pl.multiple_of(r * STEP, STEP), STEP)
                    live = (lax.broadcasted_iota(jnp.int32, (STEP, 1), 0) + r * STEP < count).astype(F32)
                    for j in range(tiles):
                        linear = jnp.dot(agg_v[here, :], weight[:, cols(j)], preferred_element_type=F32) + bias_ref[:, cols(j)].astype(F32)
                        value, factor = silu_of(linear)
                        act_v[here, cols(j)] = (value * live).astype(BF16)
                        dlin_v[here, cols(j)] = (g_v[here, cols(j)].astype(F32) * live * factor).astype(BF16)
                    for copy in outs(r):
                        copy.start()
                    for j in range(tiles):
                        dagg_v[here, cols(j)] = lax.dot_general(
                            dlin_v[here, :], weight[cols(j), :], (((1,), (1,)), ((), ())), preferred_element_type=F32
                        ).astype(BF16)

                @pl.loop(steps, slots // STEP)
                def _(r):
                    dagg_v[pl.ds(pl.multiple_of(r * STEP, STEP), STEP), :] = jnp.zeros((STEP, width), BF16)

                boundary(p, dagg_v)
                run([
                    pltpu.make_async_copy(bnd_v, send_ref.at[pl.ds(at(offset), slots)], sem.at[0]),
                    pltpu.make_async_copy(bnd_v, bnd_ref.at[slot], sem.at[2]),
                ])

                @pl.loop(0, steps)
                def _(r):
                    for copy in outs(r):
                        copy.wait()

        out_chunk = tick + 1 - lag

        @pl.when((out_chunk >= 0) & (tick + 1 < chunks))
        def _():
            run([pltpu.make_async_copy(send_ref.at[pl.ds(at(start + out_chunk * CHUNK), CHUNK)], next_ref, sem.at[0])])

    pl.when(first_section)(first)
    pl.when(jnp.logical_not(first_section))(second)


def run_tick(tick, plan, section_rows, ahat, weight, bias, got, state, packed):
    clusters, slots, width = section_rows.shape
    state_shapes = tuple(jax.ShapeDtypeStruct(s.shape, s.dtype) for s in state)
    cluster = pltpu.VMEM((slots, width), BF16)
    chunk32 = pltpu.VMEM((CHUNK, width), F32)
    outs = pl.pallas_call(
        functools.partial(tick_kernel, clusters, slots, width, packed),
        out_shape=(jax.ShapeDtypeStruct((CHUNK, width), BF16),) + state_shapes,
        in_specs=[SMEM, SMEM, ANY, ANY, ANY, VMEM, ANY] + [ANY] * 8,
        out_specs=(ANY,) * 9,
        input_output_aliases={7 + i: 1 + i for i in range(8)},
        scratch_shapes=[
            pltpu.VMEM((width, width), BF16),
            pltpu.VMEM((slots + 2 * CHUNK, slots), BF16),
            cluster, cluster, cluster, cluster, cluster, cluster, cluster, chunk32, chunk32,
            pltpu.SemaphoreType.DMA,
            pltpu.SemaphoreType.DMA,
            pltpu.SemaphoreType.DMA((3,)),
            pltpu.SemaphoreType.DMA((3,)),
            pltpu.SemaphoreType.DMA,
        ],
        compiler_params=pltpu.CompilerParams(vmem_limit_bytes=48 << 20, has_side_effects=True),
        cost_estimate=pl.CostEstimate(flops=6 * CHUNK * width * width, bytes_accessed=2 * width * width, transcendentals=0),
    )(tick, plan, section_rows, ahat, weight, bias, got, *state)
    return outs[0], outs[1:]


def finish_kernel(
    n, bits, block, nb, rows, back,
    agg_ref, dlin_ref, dfac_ref, send_ref, weight_ref, out_ref, db_ref, dagg_ref,
    agg, dlin, acc, sbuf, rbuf, res, got, dfac, dsend, drecv, dacc, dagg_v,
    lsem, wsem, bsem, osem, ssem, rsem, gssem, grsem, dssem, drsem, xssem, xrsem,
):
    width = dlin.shape[1]
    slots = acc.shape[0]
    section = lax.axis_index("section")
    me = lax.axis_index("dp")
    orders = [tuple(range(bits))] * nb
    late = pl.ds(rows - back, back)

    def bit_of(q):
        return (me // 2**q) % 2

    def partner(q):
        return (section, me + (1 - 2 * bit_of(q)) * 2**q)

    across = (1 - section, me)
    barrier = pltpu.get_barrier_semaphore()
    for q in range(bits):
        pl.semaphore_signal(barrier, inc=1, device_id=partner(q), device_id_type=MESH)
    pl.semaphore_signal(barrier, inc=1, device_id=across, device_id_type=MESH)
    load_dlin = pltpu.make_async_copy(dlin_ref.at[pl.ds(0, rows)], dlin, lsem.at[0])
    load_agg = pltpu.make_async_copy(agg_ref.at[pl.ds(0, rows)], agg, lsem.at[1])
    load_weight = pltpu.make_async_copy(weight_ref, agg, wsem)
    load_dlin.start()
    load_agg.start()
    pl.semaphore_wait(barrier, bits + 1)

    def columns(b):
        return pl.ds(b * block, block)

    def drain(b):
        return pltpu.make_async_remote_copy(
            src_ref=send_ref.at[late, columns(b)], dst_ref=got.at[b], send_sem=xssem.at[b], recv_sem=xrsem.at[b],
            device_id=across, device_id_type=MESH)

    def load_dfac(b):
        return pltpu.make_async_copy(dfac_ref.at[late, columns(b)], dfac.at[b % 2], bsem.at[b % 2])

    @pl.when(section == 1)
    def _():
        for b in range(min(2, nb)):
            drain(b).start()

    @pl.when(section == 0)
    def _():
        load_dfac(0).start()

    def piece(b, s):
        row, size = jnp.int32(0), rows_out
        for q in orders[b][:s]:
            size //= 2
            row = row + bit_of(q) * size
        return pl.multiple_of(row, 16)

    rows_out = acc.shape[1]

    def other(b, s):
        half = rows_out >> (s + 1)
        return pl.multiple_of(piece(b, s) + (1 - bit_of(orders[b][s])) * half, 16)

    def staged(b, s):
        return (b, pl.ds(rows_out - (rows_out >> s), rows_out >> (s + 1)))

    def rs(b, s):
        return pltpu.make_async_remote_copy(
            src_ref=sbuf.at[staged(b, s)], dst_ref=rbuf.at[staged(b, s)],
            send_sem=ssem.at[b, s], recv_sem=rsem.at[b, s], device_id=partner(orders[b][s]), device_id_type=MESH)

    def rs_start(b, s):
        sbuf[staged(b, s)] = acc[b % slots, pl.ds(other(b, s), rows_out >> (s + 1)), :].astype(BF16)
        rs(b, s).start()

    def rs_end(b, s):
        rs(b, s).wait_recv()
        acc[b % slots, pl.ds(piece(b, s + 1), rows_out >> (s + 1)), :] += rbuf[staged(b, s)].astype(F32)

    def ag(b, s, row):
        here = out_ref.at[b, pl.ds(row, rows_out >> (s + 1))]
        return pltpu.make_async_remote_copy(
            src_ref=here, dst_ref=here, send_sem=gssem.at[b, s], recv_sem=grsem.at[b, s],
            device_id=partner(orders[b][s]), device_id_type=MESH)

    def own(b):
        size = rows_out >> bits
        res[b] = acc[b % slots, pl.ds(piece(b, bits), size), :].astype(BF16)
        copy = pltpu.make_async_copy(res.at[b], out_ref.at[b, pl.ds(piece(b, bits), size)], osem)
        copy.start()
        copy.wait()

    def product(b):
        if b == 0:
            load_dlin.wait()
            load_agg.wait()

        @pl.when(section == 1)
        def _():
            drain(b).wait_send()
            if b + 2 < nb:
                drain(b + 2).start()

        @pl.when(section == 0)
        def _():
            load_dfac(b).wait()
            if b + 1 < nb:
                load_dfac(b + 1).start()
            drain(b).wait_recv()
            dlin[late, columns(b)] = (got[b].astype(F32) * dfac[b % 2]).astype(BF16)

        d = dlin[:, columns(b)]
        acc[b % slots] = lax.dot_general(agg[...], d, (((0,), (0,)), ((), ())), preferred_element_type=F32)
        dacc[:, columns(b)] = jnp.dot(jnp.ones((16, rows), BF16), d, preferred_element_type=F32)[:8]

    def stage(b, k):
        if k == 0:
            product(b)
            rs_start(b, 0)
        elif k < bits:
            rs_end(b, k - 1)
            rs_start(b, k)
        elif k == bits:
            rs_end(b, k - 1)
            own(b)
            ag(b, bits - 1, piece(b, bits)).start()
        else:
            s = 2 * bits - k
            ag(b, s, other(b, s)).wait_recv()
            if s > 0:
                ag(b, s - 1, piece(b, s)).start()

    def db(s):
        return pltpu.make_async_remote_copy(
            src_ref=dsend.at[s], dst_ref=drecv.at[s], send_sem=dssem.at[s], recv_sem=drsem.at[s],
            device_id=partner(s), device_id_type=MESH)

    def db_step(s):
        if s > 0:
            db(s - 1).wait_recv()
            dacc[...] += drecv[s - 1]
        if s < bits:
            dsend[s] = dacc[...]
            db(s).start()

    parts = back // 256

    def dagg_part(i):
        @pl.when(section == 0)
        def _():
            if i == 0:
                load_weight.wait()
            first = rows - back + i * 256
            for j in range(0, width, 1024):
                dagg_v[i % 2, :, j:j + 1024] = lax.dot_general(
                    dlin[pl.ds(first, 256), :], agg[pl.ds(j, 1024), :], (((1,), (1,)), ((), ())), preferred_element_type=F32
                ).astype(BF16)
            copy = pltpu.make_async_copy(dagg_v.at[i % 2], dagg_ref.at[pl.ds(i * 256, 256)], lsem.at[0])
            copy.start()
            copy.wait()

    stages = 2 * bits + 1
    for step in range(nb + stages - 1):
        for k in reversed(range(stages)):
            b = step - k
            if 0 <= b < nb:
                stage(b, k)
        if step == nb - 1:
            @pl.when(section == 0)
            def _():
                load_weight.start()
        i = step - nb
        if 0 <= i <= bits:
            db_step(i)
        if 0 <= i < parts:
            dagg_part(i)
    db_ref[...] = dacc[...]
    for b in range(nb):
        for s in range(bits):
            rs(b, s).wait_send()
            ag(b, s, piece(b, s + 1)).wait_send()
    for s in range(bits):
        db(s).wait_send()


def finish(n, agg, dlin, dfac, send, weight, rows, back):
    width = weight.shape[1]
    bits = n.bit_length() - 1
    block = 256
    nb = width // block
    slots = min(nb, bits + 1)
    rows_out = weight.shape[0]
    dma = pltpu.SemaphoreType.DMA
    return pl.pallas_call(
        functools.partial(finish_kernel, n, bits, block, nb, rows, back),
        out_shape=(
            jax.ShapeDtypeStruct((nb, rows_out, block), BF16),
            jax.ShapeDtypeStruct((8, width), F32),
            jax.ShapeDtypeStruct((back, width), BF16),
        ),
        in_specs=[ANY] * 5,
        out_specs=(ANY, VMEM, ANY),
        scratch_shapes=[
            pltpu.VMEM((rows, rows_out), BF16),
            pltpu.VMEM((rows, width), BF16),
            pltpu.VMEM((slots, rows_out, block), F32),
            pltpu.VMEM((nb, rows_out, block), BF16),
            pltpu.VMEM((nb, rows_out, block), BF16),
            pltpu.VMEM((nb, rows_out >> bits, block), BF16),
            pltpu.VMEM((nb, back, block), BF16),
            pltpu.VMEM((2, back, block), F32),
            pltpu.VMEM((bits, 8, width), F32),
            pltpu.VMEM((bits, 8, width), F32),
            pltpu.VMEM((8, width), F32),
            pltpu.VMEM((2, 256, width), BF16),
            dma((2,)), dma, dma((2,)), dma,
            dma((nb, bits)), dma((nb, bits)), dma((nb, bits)), dma((nb, bits)),
            dma((bits,)), dma((bits,)), dma((nb,)), dma((nb,)),
        ],
        compiler_params=pltpu.CompilerParams(collective_id=1, has_side_effects=True, vmem_limit_bytes=62 << 20),
        cost_estimate=pl.CostEstimate(flops=2 * rows * rows_out * width, bytes_accessed=rows * width * 8, transcendentals=0),
    )(agg, dlin, dfac, send, weight)


def closing_kernel(clusters, slots, packed, back, plan_ref, blocks_ref, ahat_ref, dagg_ref, late_ref, bnd_i, grad_ref, bnd_ref, ahat, source, bnd_v, sem, osem):
    step = pl.program_id(0)
    first_section = lax.axis_index("section") == 0
    low = packed - back - slots
    loads = [
        pltpu.make_async_copy(dagg_ref.at[pl.ds(low, slots)], source.at[pl.ds(0, slots)], sem.at[0]),
        pltpu.make_async_copy(late_ref, source.at[pl.ds(slots, back)], sem.at[1]),
    ]

    def load_ahat(p):
        return pltpu.make_async_copy(ahat_ref.at[plan_ref[SLOT, p]], ahat.at[p % 2], sem.at[2 + p % 2])

    def late(p):
        return first_section & (p < clusters) & (plan_ref[OFFSET, p] + plan_ref[COUNT, p] > packed - back)

    def store(p):
        return pltpu.make_async_copy(bnd_v.at[p % 2], bnd_ref.at[plan_ref[SLOT, p]], osem.at[p % 2])

    @pl.when(first_section & (step == 0))
    def _():
        for load in loads:
            load.start()
        source[pl.ds(slots + back, slots), :] = jnp.zeros((slots, source.shape[1]), BF16)

    for p in range(clusters):
        @pl.when((step == p) & late(p))
        def _():
            load_ahat(p).start()

    grad_ref[...] = blocks_ref[0].astype(F32)

    @pl.when(first_section & (step == 0))
    def _():
        for load in loads:
            load.wait()

    for p in range(clusters):
        @pl.when((step == p) & late(p))
        def _():
            load_ahat(p).wait()
            rows = pl.ds(pl.multiple_of(plan_ref[OFFSET, p] - low, GROUP), slots)
            for j in range(0, source.shape[1], TILE):
                bnd_v[p % 2, :, j:j + TILE] = lax.dot_general(
                    ahat[p % 2], source[rows, j:j + TILE], (((0,), (0,)), ((), ())), preferred_element_type=F32
                ).astype(BF16)
            store(p).start()

        @pl.when((step == p + 1) & late(p))
        def _():
            store(p).wait()


def closing(plan, blocks, ahat, dagg, late, bnd, packed):
    nb, rows, block = blocks.shape
    clusters, slots, width = bnd.shape
    back = late.shape[0]
    steps = max(nb, clusters + 1)
    cluster = pltpu.VMEM((2, slots, width), BF16)
    return pl.pallas_call(
        functools.partial(closing_kernel, clusters, slots, packed, back),
        grid=(steps,),
        out_shape=(jax.ShapeDtypeStruct((rows, nb * block), F32), jax.ShapeDtypeStruct(bnd.shape, BF16)),
        in_specs=[SMEM, pl.BlockSpec((1, rows, block), lambda b: (jnp.minimum(b, nb - 1), 0, 0))] + [ANY] * 4,
        out_specs=(pl.BlockSpec((rows, block), lambda b: (0, jnp.minimum(b, nb - 1))), ANY),
        input_output_aliases={5: 1},
        scratch_shapes=[
            pltpu.VMEM((2, slots, slots), BF16),
            pltpu.VMEM((2 * slots + back, width), BF16),
            cluster,
            pltpu.SemaphoreType.DMA((4,)),
            pltpu.SemaphoreType.DMA((2,)),
        ],
        compiler_params=pltpu.CompilerParams(vmem_limit_bytes=48 << 20, has_side_effects=True),
    )(plan, blocks, ahat, dagg, late, bnd)


def per_device(section_inputs, neighbours, counts, weight, bias):
    section_rows = section_inputs[0]
    weight_one = weight[0]
    clusters, slots, width = section_rows.shape
    packed = clusters * slots
    back = lag_of(slots) * CHUNK
    ahat, plan, *state = prepare(counts, neighbours, width, packed, slots)
    state = tuple(state)
    swap = [(0, 1), (1, 0)]

    def step(tick, got, state):
        return run_tick(tick, plan, section_rows, ahat, weight_one, bias, got, state, packed)

    first = jnp.full((1,), -1, jnp.int32)
    send, state = step(first, weight_one, state)

    def more(carry):
        return carry[0][0] < plan[REST, CHUNKS]

    def body(carry):
        tick, send, got, state = carry
        arrives = lax.ppermute(send, "section", swap)
        send, state = step(tick, got, state)
        return tick + 1, send, arrives, state

    tick, send, got, state = lax.while_loop(more, body, (first + 1, send, send, state))
    last, state = step(tick, got, state)
    agg, dlin, dfac, to_send, recv, dagg, act, bnd = state
    blocks, grad_bias, late = finish(lax.axis_size("dp"), agg, dlin, dfac, to_send, weight_one, packed, back)
    grad_weight, bnd = closing(plan, blocks, ahat, dagg, late, bnd, packed)
    return act[None], bnd[None], grad_weight[None], grad_bias[:1]


def solution(mesh):
    return jax.shard_map(
        per_device,
        mesh=mesh,
        in_specs=(
            P("section", "dp", None, None),
            P("dp", None, None),
            P("dp"),
            P("section", None, None),
            P("section", None),
        ),
        out_specs=(
            P("section", "dp", None, None),
            P("section", "dp", None, None),
            P("section", None, None),
            P("section", None),
        ),
        check_vma=False,
    )
```

```python
import functools

import jax
import jax.numpy as jnp
from jax import lax
from jax.experimental import pallas as pl
from jax.experimental.pallas import tpu as pltpu
from jax.sharding import PartitionSpec as P

MESH = pl.DeviceIdType.MESH
ANY = pl.BlockSpec(memory_space=pl.ANY)
HBM = pl.BlockSpec(memory_space=pltpu.MemorySpace.HBM)
SMEM = pl.BlockSpec(memory_space=pltpu.SMEM)
VMEM = pl.BlockSpec(memory_space=pltpu.VMEM)
F32, BF16 = jnp.float32, jnp.bfloat16

CHUNK = 128
STEP = 256
GROUP = 16
TILE = 1024
COUNT, OFFSET, SLOT, REST = 0, 1, 2, 3
CHUNKS = 0


def lag_of(slots):
    return (slots - 1 + CHUNK - 1) // CHUNK + 3


def up(x, by):
    return (x + by - 1) // by * by


def prepare_kernel(
    clusters, slots, packed, counts_ref, neighbours_ref,
    ahat_ref, plan_ref, agg_ref, dlin_ref, dfac_ref, send_ref, recv_ref, dagg_ref, act_ref, bnd_ref,
    zeros, zeros32, sem,
):
    c = pl.program_id(0)
    counts = [counts_ref[i] for i in range(clusters)]
    total = sum(up(n, GROUP) for n in counts)
    chunks = (total + CHUNK - 1) // CHUNK
    start = packed - chunks * CHUNK
    front = (start + CHUNK) // CHUNK
    backlog = packed // CHUNK - lag_of(slots)

    def each(act):
        for ref, first in ((agg_ref, 0), (dlin_ref, 0), (send_ref, jnp.minimum(front - 1, backlog))):
            @pl.loop(first, front)
            def _(i):
                act(pltpu.make_async_copy(zeros, ref.at[pl.ds(pl.multiple_of(i * CHUNK, CHUNK), CHUNK)], sem))

        @pl.loop(backlog, front)
        def _(i):
            act(pltpu.make_async_copy(zeros32, dfac_ref.at[pl.ds(pl.multiple_of(i * CHUNK, CHUNK), CHUNK)], sem))

        for i in range(clusters):
            @pl.loop((counts[i] + GROUP - 1) // GROUP, slots // GROUP)
            def _(g):
                rows = pl.ds(pl.multiple_of(g * GROUP, GROUP), GROUP)
                act(pltpu.make_async_copy(zeros.at[pl.ds(0, GROUP)], act_ref.at[i, rows], sem))

    @pl.when(c == 0)
    def _():
        zeros[...] = jnp.zeros_like(zeros)
        zeros32[...] = jnp.zeros_like(zeros32)
        each(lambda copy: copy.start())
        for i in range(clusters):
            rank = 0
            for j in range(clusters):
                ahead = counts[j] >= counts[i] if j < i else counts[j] > counts[i]
                rank = rank + (ahead.astype(jnp.int32) if j != i else 0)
            plan_ref[COUNT, rank] = counts[i]
            plan_ref[SLOT, rank] = i
        offset = packed - total
        for i in range(clusters):
            plan_ref[OFFSET, i] = offset
            offset = offset + up(plan_ref[COUNT, i], GROUP)
        plan_ref[REST, CHUNKS] = chunks

    count = counts_ref[c]
    slots_each = neighbours_ref.shape[2]
    group = 64

    @pl.loop(0, slots // group)
    def _(g):
        rows = pl.ds(pl.multiple_of(g * group, group), group)
        neighbours = neighbours_ref[0, rows, :]
        times = jnp.floor((neighbours.astype(F32) + 0.5) / count.astype(F32)).astype(jnp.int32)
        targets = neighbours - times * count
        columns = lax.broadcasted_iota(jnp.int32, (group, slots), 1)
        row_ids = lax.broadcasted_iota(jnp.int32, (group, slots), 0) + g * group
        adjacency = jnp.zeros((group, slots), F32)
        for k in range(slots_each):
            adjacency = adjacency + jnp.where(targets[:, k:k + 1] == columns, 1.0, 0.0)
        a = jnp.where(row_ids == columns, 2.0 * adjacency + 2.0, adjacency) / (1.0 + slots_each)
        ahat_ref[0, rows, :] = jnp.where(row_ids < count, a, 0.0).astype(BF16)

    @pl.when(c == clusters - 1)
    def _():
        each(lambda copy: copy.wait())


def prepare(counts, neighbours, width, packed, margin):
    clusters, slots, slots_each = neighbours.shape
    rows = jax.ShapeDtypeStruct((packed + margin, width), BF16)
    rows32 = jax.ShapeDtypeStruct((packed, width), F32)
    whole = jax.ShapeDtypeStruct((clusters, slots, width), BF16)
    return pl.pallas_call(
        functools.partial(prepare_kernel, clusters, slots, packed),
        grid=(clusters,),
        out_shape=(
            jax.ShapeDtypeStruct((clusters, slots, slots), BF16),
            jax.ShapeDtypeStruct((4, max(clusters, 4)), jnp.int32),
            rows, rows, rows32, rows, rows, rows, whole, whole,
        ),
        in_specs=[SMEM, pl.BlockSpec((1, slots, slots_each), lambda c: (c, 0, 0))],
        out_specs=(pl.BlockSpec((1, slots, slots), lambda c: (c, 0, 0)), SMEM) + (HBM,) * 8,
        scratch_shapes=[pltpu.VMEM((CHUNK, width), BF16), pltpu.VMEM((CHUNK, width), F32), pltpu.SemaphoreType.DMA],
        compiler_params=pltpu.CompilerParams(vmem_limit_bytes=60 << 20),
    )(counts, neighbours)


def tick_kernel(
    clusters, slots, width, packed,
    tick_ref, plan_ref, in_ref, ahat_ref, weight_ref, bias_ref, got_ref,
    agg_i, dlin_i, dfac_i, send_i, recv_i, dagg_i, act_i, bnd_i,
    next_ref, agg_ref, dlin_ref, dfac_ref, send_ref, recv_ref, dagg_ref, act_ref, bnd_ref,
    weight, ahat, back_ahat, rows_in, x_v, g_v, agg_v, act_v, dlin_v, dagg_v, dpart_v, bnd_v, dfac_v, dback_v,
    wsem, asem, xsem, bsem, gsem, outsem, bndsem, groupsem, nextsem,
):
    first_section = lax.axis_index("section") == 0
    tick = tick_ref[0]
    chunks = plan_ref[REST, CHUNKS]
    lag = lag_of(slots)
    start = packed - chunks * CHUNK
    tiles = width // TILE
    chunk = pl.ds(0, CHUNK)
    body = pl.ds(CHUNK, slots)

    def at(i):
        return pl.multiple_of(i, GROUP)

    def cols(j):
        return pl.ds(pl.multiple_of(j * TILE, TILE), TILE)

    def count_of(p):
        return plan_ref[COUNT, p]

    def offset_of(p):
        return plan_ref[OFFSET, p]

    def slot_of(p):
        return plan_ref[SLOT, p]

    def end_of(p):
        return offset_of(p) + count_of(p)

    def first_of(test):
        found = clusters
        for p in reversed(range(clusters)):
            found = jnp.where(test(p), p, found)
        return found

    def start_all(copies):
        for copy in copies:
            copy.start()

    def wait_all(copies):
        for copy in copies:
            copy.wait()

    def load_weight(j):
        return pltpu.make_async_copy(weight_ref.at[:, cols(j)], weight.at[:, cols(j)], wsem.at[j])

    def keep_live_rows(ref, count):
        @pl.loop(count // GROUP, slots // GROUP)
        def _(g):
            rows = pl.ds(pl.multiple_of(CHUNK + g * GROUP, GROUP), GROUP)
            live = lax.broadcasted_iota(jnp.int32, (GROUP, 1), 0) + g * GROUP < count
            ref[rows, :] = jnp.where(live, ref[rows, :].astype(F32), 0.0).astype(BF16)

    def silu_of(linear, live):
        s = (0.5 * jnp.tanh(0.5 * linear) + 0.5) * live
        value = linear * s
        return value, s + value * (1.0 - s)

    def boundary(adj, targets):
        @pl.loop(0, tiles)
        def _(j):
            bnd_v[:, cols(j)] = lax.dot_general(
                adj, dagg_v[body, cols(j)], (((0,), (0,)), ((), ())), preferred_element_type=F32
            ).astype(BF16)
            start_all(targets(j))

    def first():
        out_chunk = tick + 1
        out_row = start + out_chunk * CHUNK
        out_valid = out_chunk < chunks
        got_chunk = tick - 1 - lag
        got_row = start + got_chunk * CHUNK
        got_valid = (got_chunk >= 0) & (got_chunk < chunks)

        def used(p):
            return out_valid & (offset_of(p) < out_row + CHUNK) & (end_of(p) > out_row)

        def load(p):
            return [
                pltpu.make_async_copy(ahat_ref.at[slot_of(p)], ahat.at[p % 2, body], asem.at[p % 2]),
                pltpu.make_async_copy(in_ref.at[slot_of(p)], x_v.at[p % 2], xsem.at[p % 2]),
            ]

        def completed(p):
            return got_valid & (end_of(p) > got_row) & (end_of(p) <= got_row + CHUNK)

        def load_back(p):
            return [
                pltpu.make_async_copy(ahat_ref.at[slot_of(p)], back_ahat, bsem.at[0]),
                pltpu.make_async_copy(dagg_ref.at[pl.ds(at(offset_of(p)), slots)], dagg_v.at[body], bsem.at[1]),
            ]

        load_g = pltpu.make_async_copy(got_ref.at[chunk], g_v, gsem.at[0])
        load_d = pltpu.make_async_copy(dfac_ref.at[pl.ds(at(got_row), CHUNK)], dback_v, gsem.at[1])
        first_used = first_of(used)
        first_completed = first_of(completed)

        @pl.when(first_used < clusters)
        def _():
            start_all(load(first_used))

        @pl.when(out_valid | got_valid)
        def _():
            start_all([load_weight(j) for j in range(tiles)])

        @pl.when(got_valid)
        def _():
            start_all([load_g, load_d])

        @pl.when(first_completed < clusters)
        def _():
            start_all(load_back(first_completed))

        there = pl.ds(at(out_row), CHUNK)
        outs = [
            pltpu.make_async_copy(act_v.at[chunk], next_ref, outsem.at[0]),
            pltpu.make_async_copy(agg_v.at[chunk], agg_ref.at[there], outsem.at[1]),
            pltpu.make_async_copy(dfac_v, dfac_ref.at[there], outsem.at[2]),
        ]

        def groups(act):
            @pl.loop(0, CHUNK // GROUP)
            def _(g):
                row = out_row + g * GROUP

                @pl.loop(0, clusters)
                def _(p):
                    @pl.when((row >= offset_of(p)) & (row < end_of(p)))
                    def _():
                        act(pltpu.make_async_copy(
                            act_v.at[pl.ds(pl.multiple_of(g * GROUP, GROUP), GROUP)],
                            act_ref.at[slot_of(p), pl.ds(at(row - offset_of(p)), GROUP)],
                            groupsem,
                        ))

        @pl.when(out_valid)
        def _():
            zero = jnp.zeros((CHUNK, slots), BF16)
            for i in range(2):
                ahat[i, pl.ds(0, CHUNK), :] = zero
                ahat[i, pl.ds(CHUNK + slots, CHUNK), :] = zero
            agg_v[chunk, :] = jnp.zeros((CHUNK, width), BF16)

            @pl.loop(0, clusters)
            def _(p):
                @pl.when(used(p))
                def _():
                    after = jnp.minimum(p + 1, clusters - 1)

                    @pl.when((p + 1 < clusters) & used(after))
                    def _():
                        start_all(load(after))

                    wait_all(load(p))
                    a = ahat[p % 2, pl.ds(at(CHUNK + out_row - offset_of(p)), CHUNK), :]
                    for j in range(tiles):
                        agg_v[chunk, cols(j)] += jnp.dot(a, x_v[p % 2, :, cols(j)], preferred_element_type=F32).astype(BF16)

            row_ids = lax.broadcasted_iota(jnp.int32, (CHUNK, 1), 0) + out_row
            live = jnp.zeros((CHUNK, 1), jnp.bool_)
            for p in range(clusters):
                live = live | ((row_ids >= offset_of(p)) & (row_ids < end_of(p)))
            live = live.astype(F32)
            outs[1].start()
            for j in range(tiles):
                load_weight(j).wait()
                linear = jnp.dot(agg_v[chunk, :], weight[:, cols(j)], preferred_element_type=F32) + bias_ref[:, cols(j)].astype(F32)
                value, factor = silu_of(linear, live)
                act_v[chunk, cols(j)] = value.astype(BF16)
                dfac_v[:, cols(j)] = factor
            outs[0].start()
            outs[2].start()
            groups(lambda copy: copy.start())

        @pl.when(got_valid & jnp.logical_not(out_valid))
        def _():
            wait_all([load_weight(j) for j in range(tiles)])

        @pl.when(got_valid)
        def _():
            wait_all([load_g, load_d])
            dlin_v[chunk, :] = (g_v[...].astype(F32) * dback_v[...]).astype(BF16)
            there = pl.ds(at(got_row), CHUNK)
            backs = [
                pltpu.make_async_copy(dlin_v.at[chunk], dlin_ref.at[there], gsem.at[0]),
                pltpu.make_async_copy(dpart_v, dagg_ref.at[there], gsem.at[1]),
            ]
            backs[0].start()
            for j in range(tiles):
                dpart_v[:, cols(j)] = lax.dot_general(
                    dlin_v[chunk, :], weight[cols(j), :], (((1,), (1,)), ((), ())), preferred_element_type=F32
                ).astype(BF16)

            @pl.loop(0, clusters)
            def _(p):
                @pl.when(completed(p))
                def _():
                    @pl.when(p != first_completed)
                    def _():
                        start_all(load_back(p))

                    wait_all(load_back(p))
                    dagg_v[pl.ds(at(CHUNK + got_row - offset_of(p)), CHUNK), :] = dpart_v[...]
                    keep_live_rows(dagg_v, count_of(p))

                    def targets(j):
                        return [pltpu.make_async_copy(bnd_v.at[:, cols(j)], bnd_ref.at[slot_of(p), :, cols(j)], bndsem.at[0, j])]

                    boundary(back_ahat[...], targets)
                    for j in range(tiles):
                        wait_all(targets(j))

            backs[1].start()
            wait_all(backs)

        @pl.when(out_valid)
        def _():
            wait_all(outs)
            groups(lambda copy: copy.wait())

    def second():
        got_chunk = tick - 1
        got_row = start + got_chunk * CHUNK
        got_valid = (got_chunk >= 0) & (got_chunk < chunks)
        out_chunk = tick + 1 - lag
        out_row = start + out_chunk * CHUNK
        out_valid = (out_chunk >= 0) & (tick < chunks)

        def ends_in(p, row):
            return (end_of(p) > row) & (end_of(p) <= row + CHUNK)

        def splits(p, row):
            after = jnp.where(p + 1 < clusters, end_of(jnp.minimum(p + 1, clusters - 1)), row + 2 * CHUNK)
            return (count_of(p) > STEP) & ends_in(p, row) & (after > row + CHUNK)

        def fresh(p):
            return got_valid & ends_in(p, got_row)

        def begun(p):
            return (got_chunk > 0) & splits(p, got_row - CHUNK)

        def task(p):
            return fresh(p) | begun(p)

        def load(p):
            return [
                pltpu.make_async_copy(recv_ref.at[pl.ds(at(offset_of(p)), slots)], rows_in.at[body], xsem.at[0]),
                pltpu.make_async_copy(ahat_ref.at[slot_of(p)], back_ahat, asem.at[0]),
            ]

        def load_begun(p):
            return [
                pltpu.make_async_copy(agg_ref.at[pl.ds(at(offset_of(p) + STEP), slots - STEP)], agg_v.at[pl.ds(STEP, slots - STEP)], xsem.at[0]),
                pltpu.make_async_copy(ahat_ref.at[slot_of(p)], back_ahat, asem.at[0]),
                pltpu.make_async_copy(dagg_ref.at[pl.ds(at(offset_of(p)), STEP)], dagg_v.at[pl.ds(CHUNK, STEP)], asem.at[1]),
            ]

        def load_g(p):
            return pltpu.make_async_copy(in_ref.at[slot_of(p)], x_v.at[0], xsem.at[1])

        def start_loads(p):
            @pl.when(fresh(p))
            def _():
                start_all(load(p))

            @pl.when(jnp.logical_not(fresh(p)))
            def _():
                start_all(load_begun(p))

            load_g(p).start()

        load_got = pltpu.make_async_copy(got_ref.at[chunk], g_v, gsem.at[0])
        keep_got = pltpu.make_async_copy(got_ref.at[chunk], recv_ref.at[pl.ds(at(got_row), CHUNK)], gsem.at[1])
        put_next = pltpu.make_async_copy(send_ref.at[pl.ds(at(out_row), CHUNK)], next_ref, nextsem)
        first_task = first_of(task)
        some = first_task < clusters
        new = out_valid & some & (offset_of(jnp.minimum(first_task, clusters - 1)) < out_row + CHUNK)

        @pl.when(some)
        def _():
            start_loads(first_task)
            start_all([load_weight(j) for j in range(tiles)])

        @pl.when(got_valid)
        def _():
            load_got.start()

        @pl.when(out_valid & jnp.logical_not(new))
        def _():
            put_next.start()

        @pl.when(got_valid)
        def _():
            load_got.wait()

        @pl.loop(0, clusters)
        def _(p):
            @pl.when(task(p))
            def _():
                offset, count, slot = offset_of(p), count_of(p), slot_of(p)
                steps = (count + STEP - 1) // STEP
                is_fresh = fresh(p)
                partial = is_fresh & splits(p, got_row) & (tick < chunks)

                @pl.when(p != first_task)
                def _():
                    start_loads(p)

                def keep_agg(r):
                    here = pl.ds(pl.multiple_of(r * STEP, STEP), STEP)
                    return pltpu.make_async_copy(agg_v.at[here], agg_ref.at[pl.ds(at(offset + r * STEP), STEP)], outsem.at[0])

                @pl.when(is_fresh)
                def _():
                    wait_all(load(p))
                    rows_in[pl.ds(at(CHUNK + got_row - offset), CHUNK), :] = g_v[...]
                    keep_live_rows(rows_in, count)

                    @pl.loop(0, tiles)
                    def _(j):
                        agg_v[:, cols(j)] = jnp.dot(back_ahat[...], rows_in[body, cols(j)], preferred_element_type=F32).astype(BF16)

                    @pl.loop(0, steps)
                    def _(r):
                        keep_agg(r).start()

                @pl.when(jnp.logical_not(is_fresh))
                def _():
                    wait_all(load_begun(p))

                load_g(p).wait()

                @pl.when(p == first_task)
                def _():
                    wait_all([load_weight(j) for j in range(tiles)])

                def outs(r):
                    here = pl.ds(pl.multiple_of(r * STEP, STEP), STEP)
                    there = pl.ds(at(offset + r * STEP), STEP)
                    return [
                        pltpu.make_async_copy(act_v.at[here], act_ref.at[slot, here], outsem.at[1]),
                        pltpu.make_async_copy(dlin_v.at[here], dlin_ref.at[there], outsem.at[2]),
                    ]

                first_step = jnp.where(is_fresh, 0, 1)
                last_step = jnp.where(partial, 1, steps)

                @pl.loop(first_step, last_step)
                def _(r):
                    here = pl.ds(pl.multiple_of(r * STEP, STEP), STEP)
                    live = (lax.broadcasted_iota(jnp.int32, (STEP, 1), 0) + r * STEP < count).astype(F32)

                    @pl.loop(0, tiles)
                    def _(j):
                        linear = jnp.dot(agg_v[here, :], weight[:, cols(j)], preferred_element_type=F32) + bias_ref[:, cols(j)].astype(F32)
                        value, factor = silu_of(linear, live)
                        act_v[here, cols(j)] = value.astype(BF16)
                        dlin_v[here, cols(j)] = (x_v[0, here, cols(j)].astype(F32) * factor).astype(BF16)

                    start_all(outs(r))

                    @pl.loop(0, tiles)
                    def _(j):
                        dagg_v[pl.ds(pl.multiple_of(CHUNK + r * STEP, CHUNK), STEP), cols(j)] = lax.dot_general(
                            dlin_v[here, :], weight[cols(j), :], (((1,), (1,)), ((), ())), preferred_element_type=F32
                        ).astype(BF16)

                keep_dagg = pltpu.make_async_copy(dagg_v.at[pl.ds(CHUNK, STEP)], dagg_ref.at[pl.ds(at(offset), STEP)], asem.at[1])

                @pl.when(partial)
                def _():
                    keep_dagg.start()
                    keep_dagg.wait()

                @pl.when(jnp.logical_not(partial))
                def _():
                    @pl.loop(steps, slots // STEP)
                    def _(r):
                        dagg_v[pl.ds(pl.multiple_of(CHUNK + r * STEP, CHUNK), STEP), :] = jnp.zeros((STEP, width), BF16)

                    def targets(j):
                        return [
                            pltpu.make_async_copy(bnd_v.at[:, cols(j)], send_ref.at[pl.ds(at(offset), slots), cols(j)], bndsem.at[0, j]),
                            pltpu.make_async_copy(bnd_v.at[:, cols(j)], bnd_ref.at[slot, :, cols(j)], bndsem.at[1, j]),
                        ]

                    boundary(back_ahat[...], targets)
                    for j in range(tiles):
                        wait_all(targets(j))

                @pl.loop(first_step, last_step)
                def _(r):
                    wait_all(outs(r))

                @pl.when(is_fresh)
                def _():
                    @pl.loop(0, steps)
                    def _(r):
                        keep_agg(r).wait()

        @pl.when(got_valid)
        def _():
            keep_got.start()

        @pl.when(new)
        def _():
            put_next.start()

        @pl.when(got_valid)
        def _():
            keep_got.wait()

        @pl.when(out_valid)
        def _():
            put_next.wait()

    pl.when(first_section)(first)
    pl.when(jnp.logical_not(first_section))(second)


def run_tick(tick, plan, section_rows, ahat, weight, bias, got, state, packed):
    clusters, slots, width = section_rows.shape
    tiles = width // TILE
    state_shapes = tuple(jax.ShapeDtypeStruct(s.shape, s.dtype) for s in state)
    cluster = pltpu.VMEM((slots, width), BF16)
    roomy = pltpu.VMEM((slots + 2 * CHUNK, width), BF16)
    chunk = pltpu.VMEM((CHUNK, width), BF16)
    chunk32 = pltpu.VMEM((CHUNK, width), F32)
    dma = pltpu.SemaphoreType.DMA
    outs = pl.pallas_call(
        functools.partial(tick_kernel, clusters, slots, width, packed),
        out_shape=(jax.ShapeDtypeStruct((CHUNK, width), BF16),) + state_shapes,
        in_specs=[SMEM, SMEM, ANY, ANY, ANY, VMEM, ANY] + [HBM] * 8,
        out_specs=(ANY,) + (HBM,) * 8,
        input_output_aliases={7 + i: 1 + i for i in range(8)},
        scratch_shapes=[
            pltpu.VMEM((width, width), BF16),
            pltpu.VMEM((2, slots + 2 * CHUNK, slots), BF16),
            pltpu.VMEM((slots, slots), BF16),
            roomy,
            pltpu.VMEM((2, slots, width), BF16),
            chunk, cluster, cluster, cluster, roomy, chunk, cluster, chunk32, chunk32,
            dma((tiles,)), dma((2,)), dma((2,)), dma((2,)), dma((2,)), dma((3,)), dma((2, tiles)), dma, dma,
        ],
        compiler_params=pltpu.CompilerParams(vmem_limit_bytes=57 << 20, has_side_effects=True),
        cost_estimate=pl.CostEstimate(flops=6 * CHUNK * width * width, bytes_accessed=2 * width * width, transcendentals=0),
    )(tick, plan, section_rows, ahat, weight, bias, got, *state)
    return outs[0], outs[1:]


def tracks_of(n, rows):
    weights = [2**q for q in range(n.bit_length() - 1)]
    part = rows // 4
    if len(weights) < 3 or part // n < 16:
        return [(0, rows, weights)]
    return [(0, rows - part, weights), (rows - part, part, [weights[0], weights[2], weights[1]] + weights[3:])]


def finish_kernel(
    n, block, halves, rows, back,
    agg_ref, dlin_ref, dfac_ref, send_ref, last_ref, weight_ref, out_ref, db_ref, dagg_ref,
    agg, dlin, acc, sbuf, rbuf, res, got, dfac, dsend, drecv, dsum, dacc, dagg_v, last_v,
    lsem, wsem, bsem, osem, ssem, rsem, gssem, grsem, dssem, drsem, xssem, xrsem,
):
    width = dlin.shape[1]
    slots, rows_out = acc.shape[0], acc.shape[1]
    nb = res.shape[0]
    column_blocks = nb // halves
    section = lax.axis_index("section")
    me = lax.axis_index("dp")
    tracks = tracks_of(n, rows_out)
    depth = len(tracks[0][2])
    late = pl.ds(rows - back, back)
    drained = pl.ds(rows - back + CHUNK, back - CHUNK)
    hops = [(s, m) for s in range(depth) for m in range(len(tracks))]

    def bit(m, s):
        return (me // tracks[m][2][s]) % 2

    def partner(s, m):
        return (section, me + (1 - 2 * bit(m, s)) * tracks[m][2][s])

    across = (1 - section, me)
    barrier = pltpu.get_barrier_semaphore()
    for s in range(depth):
        pl.semaphore_signal(barrier, inc=1, device_id=partner(s, 0), device_id_type=MESH)
    pl.semaphore_signal(barrier, inc=1, device_id=across, device_id_type=MESH)
    load_dlin = pltpu.make_async_copy(dlin_ref.at[pl.ds(0, rows)], dlin, lsem.at[0])
    load_agg = pltpu.make_async_copy(agg_ref.at[pl.ds(0, rows)], agg, lsem.at[1])
    load_weight = pltpu.make_async_copy(weight_ref, agg, wsem)
    load_dlin.start()
    load_agg.start()
    pl.semaphore_wait(barrier, depth + 1)

    def columns(c):
        return pl.ds(pl.multiple_of(c * block, block), block)

    def drain(c):
        return pltpu.make_async_remote_copy(
            src_ref=send_ref.at[drained, columns(c)], dst_ref=got.at[c], send_sem=xssem.at[c], recv_sem=xrsem.at[c],
            device_id=across, device_id_type=MESH)

    def load_back(c):
        return [
            pltpu.make_async_copy(dfac_ref.at[late, columns(c)], dfac.at[c % 2], bsem.at[c % 2, 0]),
            pltpu.make_async_copy(last_ref.at[:, columns(c)], last_v.at[c % 2], bsem.at[c % 2, 1]),
        ]

    @pl.when(section == 1)
    def _():
        for c in range(min(2, column_blocks)):
            drain(c).start()

    @pl.when(section == 0)
    def _():
        for copy in load_back(0):
            copy.start()

    def size(m, s):
        return tracks[m][1] >> s

    def piece(m, s):
        row = tracks[m][0]
        for q in range(s):
            row = row + bit(m, q) * size(m, q + 1)
        return row

    def other(m, s):
        return piece(m, s) + (1 - bit(m, s)) * size(m, s + 1)

    def rows_at(row, m, s):
        return pl.ds(pl.multiple_of(row, 16), size(m, s + 1))

    def staged(m, s):
        return pl.ds(tracks[m][0] + tracks[m][1] - size(m, s), size(m, s + 1))

    def rs(b, s, m):
        return pltpu.make_async_remote_copy(
            src_ref=sbuf.at[b, staged(m, s)], dst_ref=rbuf.at[b, staged(m, s)],
            send_sem=ssem.at[b, s, m], recv_sem=rsem.at[b, s, m], device_id=partner(s, m), device_id_type=MESH)

    def rs_start(b, s):
        for m in range(len(tracks)):
            sbuf[b, staged(m, s), :] = acc[b % slots, rows_at(other(m, s), m, s), :].astype(BF16)
            rs(b, s, m).start()

    def rs_end(b, s):
        for m in range(len(tracks)):
            here = rows_at(piece(m, s + 1), m, s)
            rs(b, s, m).wait_recv()
            total = acc[b % slots, here, :] + rbuf[b, staged(m, s), :].astype(F32)
            if s + 1 < depth:
                acc[b % slots, here, :] = total
            else:
                res[b, here, :] = total.astype(BF16)

    def ag(b, s, m, row):
        here = res.at[b, rows_at(row, m, s)]
        return pltpu.make_async_remote_copy(
            src_ref=here, dst_ref=here, send_sem=gssem.at[b, s, m], recv_sem=grsem.at[b, s, m],
            device_id=partner(s, m), device_id_type=MESH)

    def ag_start(b, s):
        for m in range(len(tracks)):
            ag(b, s, m, piece(m, s + 1)).start()

    def ag_end(b, s):
        for m in range(len(tracks)):
            ag(b, s, m, other(m, s)).wait_recv()

    def out(b):
        return pltpu.make_async_copy(res.at[b], out_ref.at[b], osem.at[b])

    def product(b):
        c = b // halves

        @pl.when(b % halves == 0)
        def _():
            @pl.when(section == 1)
            def _():
                drain(c).wait_send()

                @pl.when(c + 2 < column_blocks)
                def _():
                    drain(c + 2).start()

            @pl.when(section == 0)
            def _():
                for copy in load_back(c):
                    copy.wait()

                @pl.when(c + 1 < column_blocks)
                def _():
                    for copy in load_back(c + 1):
                        copy.start()

                last = last_v[c % 2]
                factor = dfac[c % 2, pl.ds(0, CHUNK)]
                value = jnp.where(factor == 0.0, 0.0, last.astype(F32) * factor)
                dlin[pl.ds(rows - back, CHUNK), columns(c)] = value.astype(BF16)
                drain(c).wait_recv()
                dlin[drained, columns(c)] = (got[c].astype(F32) * dfac[c % 2, pl.ds(CHUNK, back - CHUNK)]).astype(BF16)

            @pl.loop(0, rows // 256)
            def _(i):
                some = dlin[pl.ds(pl.multiple_of(i * 256, 256), 256), columns(c)].astype(F32)
                dacc[:, columns(c)] += jnp.sum(some.reshape(32, 8, block), axis=0)


        d = dlin[:, columns(c)]
        part = min(rows_out, 512 if slots < nb else 256)

        @pl.loop(0, rows_out // part)
        def _(i):
            r = pl.ds(pl.multiple_of(i * part, part), part)
            a = agg[:, pl.ds(pl.multiple_of((b % halves) * rows_out + i * part, part), part)]
            acc[b % slots, r, :] = lax.dot_general(a, d, (((0,), (0,)), ((), ())), preferred_element_type=F32)

    def stage(b, k):
        if k == 0:
            product(b)
            rs_start(b, 0)
        elif k < depth:
            rs_end(b, k - 1)
            rs_start(b, k)
        elif k == depth:
            rs_end(b, k - 1)
            ag_start(b, depth - 1)
        else:
            s = 2 * depth - k
            ag_end(b, s)
            if s > 0:
                ag_start(b, s - 1)
            else:
                out(b).start()

    bits = dsend.shape[0]

    def db(q):
        to = (section, me + (1 - 2 * ((me // 2**q) % 2)) * 2**q)
        return pltpu.make_async_remote_copy(
            src_ref=dsend.at[q], dst_ref=drecv.at[q], send_sem=dssem.at[q], recv_sem=drsem.at[q],
            device_id=to, device_id_type=MESH)

    def db_step(q):
        if q == 0:
            whole = jnp.sum(dacc[...], axis=0, keepdims=True)
            for i in range(8):
                dsum[i:i + 1, :] = whole[:, i * (width // 8):(i + 1) * (width // 8)]
        else:
            db(q - 1).wait_recv()
            dsum[...] += drecv[q - 1]
        if q < bits:
            dsend[q] = dsum[...]
            db(q).start()

    parts = back // dagg_v.shape[0]

    def dagg_part(i):
        size = dagg_v.shape[0]
        first = pl.multiple_of(rows - back + i * size, 32)

        @pl.loop(0, width // 512)
        def _(j):
            c = pl.ds(pl.multiple_of(j * 512, 512), 512)
            dagg_v[:, c] = lax.dot_general(
                dlin[pl.ds(first, size), :], agg[c, :], (((1,), (1,)), ((), ())), preferred_element_type=F32
            ).astype(BF16)

        copy = pltpu.make_async_copy(dagg_v, dagg_ref.at[pl.ds(pl.multiple_of(i * size, 32), size)], lsem.at[0])
        copy.start()
        copy.wait()

    dacc[...] = jnp.zeros_like(dacc)
    load_dlin.wait()
    load_agg.wait()
    stages = 2 * depth + 1

    @pl.loop(0, nb + stages - 1)
    def _(step):
        for k in reversed(range(stages)):
            b = step - k

            @pl.when((b >= 0) & (b < nb))
            def _():
                stage(b, k)

        @pl.when((step == nb - 1) & (section == 0))
        def _():
            load_weight.start()

        for q in range(min(bits + 1, stages - 1)):
            @pl.when(step == nb + q)
            def _():
                db_step(q)

        @pl.when((step == nb) & (section == 0))
        def _():
            load_weight.wait()

        @pl.when((step >= nb) & (step < nb + parts) & (section == 0))
        def _():
            dagg_part(step - nb)

    for q in range(min(bits + 1, stages - 1), bits + 1):
        db_step(q)
    db_ref[...] = dsum[...]

    @pl.loop(0, nb)
    def _(b):
        for s, m in hops:
            rs(b, s, m).wait_send()
            ag(b, s, m, piece(m, s + 1)).wait_send()
        out(b).wait()

    for q in range(bits):
        db(q).wait_send()


def finish(n, agg, dlin, dfac, send, last, weight, rows, back):
    width = weight.shape[1]
    bits = n.bit_length() - 1
    block = 256
    halves = 1
    rows_out = weight.shape[0] // halves
    column_blocks = width // block
    nb = column_blocks * halves
    slots = min(nb, bits + 1)
    tracks = len(tracks_of(n, rows_out))
    dma = pltpu.SemaphoreType.DMA
    return pl.pallas_call(
        functools.partial(finish_kernel, n, block, halves, rows, back),
        out_shape=(
            jax.ShapeDtypeStruct((nb, rows_out, block), BF16),
            jax.ShapeDtypeStruct((8, width // 8), F32),
            jax.ShapeDtypeStruct((back, width), BF16),
        ),
        in_specs=[ANY] * 6,
        out_specs=(ANY, VMEM, ANY),
        scratch_shapes=[
            pltpu.VMEM((rows, weight.shape[0]), BF16),
            pltpu.VMEM((rows, width), BF16),
            pltpu.VMEM((slots, rows_out, block), F32),
            pltpu.VMEM((nb, rows_out, block), BF16),
            pltpu.VMEM((nb, rows_out, block), BF16),
            pltpu.VMEM((nb, rows_out, block), BF16),
            pltpu.VMEM((column_blocks, back - CHUNK, block), BF16),
            pltpu.VMEM((2, back, block), F32),
            pltpu.VMEM((bits, 8, width // 8), F32),
            pltpu.VMEM((bits, 8, width // 8), F32),
            pltpu.VMEM((8, width // 8), F32),
            pltpu.VMEM((8, width), F32),
            pltpu.VMEM((back // 4, width), BF16),
            pltpu.VMEM((2, CHUNK, block), BF16),
            dma((2,)), dma, dma((2, 2)), dma((nb,)),
            dma((nb, bits, tracks)), dma((nb, bits, tracks)), dma((nb, bits, tracks)), dma((nb, bits, tracks)),
            dma((bits,)), dma((bits,)), dma((column_blocks,)), dma((column_blocks,)),
        ],
        compiler_params=pltpu.CompilerParams(collective_id=1, has_side_effects=True, vmem_limit_bytes=63 << 20),
        cost_estimate=pl.CostEstimate(flops=2 * rows * weight.shape[0] * width, bytes_accessed=rows * width * 8, transcendentals=0),
    )(agg, dlin, dfac, send, last, weight)


def closing_kernel(
    clusters, slots, packed, back, plan_ref, blocks_ref, sums_ref, ahat_ref, dagg_ref, late_ref, bnd_i,
    grad_ref, bias_ref, bnd_ref, ahat, source, bnd_v, sem, asem, osem,
):
    step = pl.program_id(0)
    first_section = lax.axis_index("section") == 0
    low = packed - back - slots
    loads = [
        pltpu.make_async_copy(dagg_ref.at[pl.ds(low, slots)], source.at[pl.ds(0, slots)], sem.at[0]),
        pltpu.make_async_copy(late_ref, source.at[pl.ds(slots, back)], sem.at[1]),
    ]

    def load_ahat(p):
        return pltpu.make_async_copy(ahat_ref.at[plan_ref[SLOT, p]], ahat.at[p], asem.at[p])

    def late(p):
        return first_section & (plan_ref[OFFSET, p] + plan_ref[COUNT, p] > packed - back)

    def store(p):
        return pltpu.make_async_copy(bnd_v.at[p % 2], bnd_ref.at[plan_ref[SLOT, p]], osem.at[p % 2])

    @pl.when(step == 0)
    def _():
        part = sums_ref.shape[1]
        for i in range(8):
            bias_ref[:, i * part:(i + 1) * part] = sums_ref[i:i + 1, :]

    @pl.when(first_section & (step == 0))
    def _():
        for load in loads:
            load.start()
        for p in range(clusters):
            @pl.when(late(p))
            def _():
                load_ahat(p).start()
        source[pl.ds(slots + back, slots), :] = jnp.zeros((slots, source.shape[1]), BF16)

    grad_ref[...] = blocks_ref[0].astype(F32)

    @pl.when(first_section & (step == 1))
    def _():
        for load in loads:
            load.wait()

    for p in range(clusters):
        @pl.when((step == p + 1) & late(p))
        def _():
            load_ahat(p).wait()
            rows = pl.ds(pl.multiple_of(plan_ref[OFFSET, p] - low, GROUP), slots)

            @pl.loop(0, source.shape[1] // TILE)
            def _(j):
                cols = pl.ds(pl.multiple_of(j * TILE, TILE), TILE)
                bnd_v[p % 2, :, cols] = lax.dot_general(
                    ahat[p], source[rows, cols], (((0,), (0,)), ((), ())), preferred_element_type=F32
                ).astype(BF16)

            store(p).start()

        @pl.when((step == p + 2) & late(p))
        def _():
            store(p).wait()


def closing(plan, blocks, sums, ahat, dagg, late, bnd, packed):
    nb, rows, block = blocks.shape
    clusters, slots, width = bnd.shape
    halves = nb * block // width
    back = late.shape[0]
    steps = max(nb, clusters + 2)
    return pl.pallas_call(
        functools.partial(closing_kernel, clusters, slots, packed, back),
        grid=(steps,),
        out_shape=(
            jax.ShapeDtypeStruct((rows * halves, width), F32),
            jax.ShapeDtypeStruct((1, width), F32),
            jax.ShapeDtypeStruct(bnd.shape, BF16),
        ),
        in_specs=[SMEM, pl.BlockSpec((1, rows, block), lambda b: (jnp.minimum(b, nb - 1), 0, 0)), VMEM] + [ANY] * 4,
        out_specs=(
            pl.BlockSpec((rows, block), lambda b: (jnp.minimum(b, nb - 1) % halves, jnp.minimum(b, nb - 1) // halves)),
            pl.BlockSpec((1, width), lambda b: (0, 0)),
            ANY,
        ),
        input_output_aliases={6: 2},
        scratch_shapes=[
            pltpu.VMEM((clusters, slots, slots), BF16),
            pltpu.VMEM((2 * slots + back, width), BF16),
            pltpu.VMEM((2, slots, width), BF16),
            pltpu.SemaphoreType.DMA((2,)),
            pltpu.SemaphoreType.DMA((clusters,)),
            pltpu.SemaphoreType.DMA((2,)),
        ],
        compiler_params=pltpu.CompilerParams(vmem_limit_bytes=60 << 20, has_side_effects=True),
    )(plan, blocks, sums, ahat, dagg, late, bnd)


def per_device(section_inputs, neighbours, counts, weight, bias):
    section_rows = section_inputs[0]
    weight_one = weight[0]
    clusters, slots, width = section_rows.shape
    packed = clusters * slots
    back = lag_of(slots) * CHUNK
    ahat, plan, *state = prepare(counts, neighbours, width, packed, slots)
    state = tuple(state)
    swap = [(0, 1), (1, 0)]

    def step(tick, got, state):
        return run_tick(tick, plan, section_rows, ahat, weight_one, bias, got, state, packed)

    first = jnp.full((1,), -1, jnp.int32)
    send, state = step(first, weight_one, state)
    send, last_plan = lax.optimization_barrier((send, plan))
    chunks = last_plan[REST, CHUNKS]

    def more(carry):
        return carry[0][0] <= chunks

    def body(carry):
        tick, send, got, state = carry
        arrives = lax.ppermute(send, "section", swap)
        send, state = step(tick, got, state)
        return tick + 1, send, arrives, state

    tick, send, got, state = lax.while_loop(more, body, (first + 1, send, send, state))
    agg, dlin, dfac, to_send, recv, dagg, act, bnd = state
    blocks, sums, late = finish(lax.axis_size("dp"), agg, dlin, dfac, to_send, got, weight_one, packed, back)
    grad_weight, grad_bias, bnd = closing(plan, blocks, sums, ahat, dagg, late, bnd, packed)
    return act[None], bnd[None], grad_weight[None], grad_bias


def solution(mesh):
    return jax.shard_map(
        per_device,
        mesh=mesh,
        in_specs=(
            P("section", "dp", None, None),
            P("dp", None, None),
            P("dp"),
            P("section", None, None),
            P("section", None),
        ),
        out_specs=(
            P("section", "dp", None, None),
            P("section", "dp", None, None),
            P("section", None, None),
            P("section", None),
        ),
        check_vma=False,
    )
```

```python
import functools

import jax
import jax.numpy as jnp
from jax import lax
from jax.experimental import pallas as pl
from jax.experimental.pallas import tpu as pltpu
from jax.sharding import PartitionSpec as P

MESH = pl.DeviceIdType.MESH
ANY = pl.BlockSpec(memory_space=pl.ANY)
HBM = pl.BlockSpec(memory_space=pltpu.MemorySpace.HBM)
SMEM = pl.BlockSpec(memory_space=pltpu.SMEM)
VMEM = pl.BlockSpec(memory_space=pltpu.VMEM)
F32, BF16 = jnp.float32, jnp.bfloat16

CHUNK = 128
STEP = 256
GROUP = 16
TILE = 1024
FINE = 512
COUNT, OFFSET, SLOT, REST = 0, 1, 2, 3
CHUNKS = 0


def lag_of(slots):
    return (slots - 1 + CHUNK - 1) // CHUNK + 3


def up(x, by):
    return (x + by - 1) // by * by


def prepare_kernel(
    clusters, slots, packed, counts_ref, neighbours_ref,
    ahat_ref, plan_ref, agg_ref, dlin_ref, dfac_ref, send_ref, recv_ref, dagg_ref, act_ref, bnd_ref,
    zeros, zeros32, targets, sem,
):
    c = pl.program_id(0)
    counts = [counts_ref[i] for i in range(clusters)]
    total = sum(up(n, GROUP) for n in counts)
    chunks = (total + CHUNK - 1) // CHUNK
    start = packed - chunks * CHUNK
    front = (start + CHUNK) // CHUNK
    backlog = packed // CHUNK - lag_of(slots)

    def each(act):
        for ref, first in ((agg_ref, 0), (dlin_ref, 0), (send_ref, jnp.minimum(front - 1, backlog))):
            @pl.loop(first, front)
            def _(i):
                act(pltpu.make_async_copy(zeros, ref.at[pl.ds(pl.multiple_of(i * CHUNK, CHUNK), CHUNK)], sem))

        @pl.loop(backlog, front)
        def _(i):
            act(pltpu.make_async_copy(zeros32, dfac_ref.at[pl.ds(pl.multiple_of(i * CHUNK, CHUNK), CHUNK)], sem))

        for i in range(clusters):
            @pl.loop((counts[i] + GROUP - 1) // GROUP, slots // GROUP)
            def _(g):
                rows = pl.ds(pl.multiple_of(g * GROUP, GROUP), GROUP)
                act(pltpu.make_async_copy(zeros.at[pl.ds(0, GROUP)], act_ref.at[i, rows], sem))

    @pl.when(c == 0)
    def _():
        zeros[...] = jnp.zeros_like(zeros)
        zeros32[...] = jnp.zeros_like(zeros32)
        each(lambda copy: copy.start())
        for i in range(clusters):
            rank = 0
            for j in range(clusters):
                ahead = counts[j] >= counts[i] if j < i else counts[j] > counts[i]
                rank = rank + (ahead.astype(jnp.int32) if j != i else 0)
            plan_ref[COUNT, rank] = counts[i]
            plan_ref[SLOT, rank] = i
        offset = packed - total
        for i in range(clusters):
            plan_ref[OFFSET, i] = offset
            offset = offset + up(plan_ref[COUNT, i], GROUP)
        plan_ref[REST, CHUNKS] = chunks

    count = counts_ref[c]
    slots_each = neighbours_ref.shape[1]
    neighbours = neighbours_ref[0].astype(F32)
    size = count.astype(F32)
    targets[:, 0:slots_each] = jnp.transpose(neighbours - jnp.floor((neighbours + 0.5) / size) * size)
    group = 64
    groups = (count + group - 1) // group

    @pl.loop(0, groups)
    def _(g):
        rows = pl.ds(pl.multiple_of(g * group, group), group)
        here = targets[rows, :].astype(jnp.int32)
        columns = lax.broadcasted_iota(jnp.int32, (group, slots), 1)
        row_ids = lax.broadcasted_iota(jnp.int32, (group, slots), 0) + g * group
        adjacency = jnp.zeros((group, slots), F32)
        for k in range(slots_each):
            adjacency = adjacency + jnp.where(here[:, k:k + 1] == columns, 1.0, 0.0)
        a = jnp.where(row_ids == columns, 2.0 * adjacency + 2.0, adjacency) / (1.0 + slots_each)
        ahat_ref[0, rows, :] = jnp.where(row_ids < count, a, 0.0).astype(BF16)

    @pl.loop(groups, slots // group)
    def _(g):
        ahat_ref[0, pl.ds(pl.multiple_of(g * group, group), group), :] = jnp.zeros((group, slots), BF16)

    @pl.when(c == clusters - 1)
    def _():
        each(lambda copy: copy.wait())


def prepare(counts, neighbours, width, packed, margin):
    clusters, slots_each, slots = neighbours.shape
    rows = jax.ShapeDtypeStruct((packed + margin, width), BF16)
    rows32 = jax.ShapeDtypeStruct((packed, width), F32)
    whole = jax.ShapeDtypeStruct((clusters, slots, width), BF16)
    return pl.pallas_call(
        functools.partial(prepare_kernel, clusters, slots, packed),
        grid=(clusters,),
        out_shape=(
            jax.ShapeDtypeStruct((clusters, slots, slots), BF16),
            jax.ShapeDtypeStruct((4, max(clusters, 4)), jnp.int32),
            rows, rows, rows32, rows, rows, rows, whole, whole,
        ),
        in_specs=[SMEM, pl.BlockSpec((1, slots_each, slots), lambda c: (c, 0, 0))],
        out_specs=(pl.BlockSpec((1, slots, slots), lambda c: (c, 0, 0)), SMEM) + (HBM,) * 8,
        scratch_shapes=[pltpu.VMEM((CHUNK, width), BF16), pltpu.VMEM((CHUNK, width), F32), pltpu.VMEM((slots, 128), F32), pltpu.SemaphoreType.DMA],
        compiler_params=pltpu.CompilerParams(vmem_limit_bytes=60 << 20),
    )(counts, neighbours)


def tick_kernel(
    clusters, slots, width, packed,
    tick_ref, plan_ref, in_ref, ahat_ref, weight_ref, bias_ref, got_ref,
    agg_i, dlin_i, dfac_i, send_i, recv_i, dagg_i, act_i, bnd_i,
    next_ref, agg_ref, dlin_ref, dfac_ref, send_ref, recv_ref, dagg_ref, act_ref, bnd_ref,
    weight, ahat, back_ahat, rows_in, x_v, g_v, agg_v, act_v, dlin_v, dagg_v, dpart_v, bnd_v, dfac_v, dback_v,
    wsem, asem, xsem, bsem, gsem, outsem, bndsem, groupsem, nextsem,
):
    first_section = lax.axis_index("section") == 0
    tick = tick_ref[0]
    chunks = plan_ref[REST, CHUNKS]
    lag = lag_of(slots)
    start = packed - chunks * CHUNK
    tiles = width // TILE
    chunk = pl.ds(0, CHUNK)
    body = pl.ds(CHUNK, slots)

    def at(i):
        return pl.multiple_of(i, GROUP)

    def cols(j):
        return pl.ds(pl.multiple_of(j * TILE, TILE), TILE)

    def fine(j):
        return pl.ds(pl.multiple_of(j * FINE, FINE), FINE)

    def count_of(p):
        return plan_ref[COUNT, p]

    def offset_of(p):
        return plan_ref[OFFSET, p]

    def slot_of(p):
        return plan_ref[SLOT, p]

    def end_of(p):
        return offset_of(p) + count_of(p)

    def first_of(test):
        found = clusters
        for p in reversed(range(clusters)):
            found = jnp.where(test(p), p, found)
        return found

    def start_all(copies):
        for copy in copies:
            copy.start()

    def wait_all(copies):
        for copy in copies:
            copy.wait()

    def load_weight(j):
        return pltpu.make_async_copy(weight_ref.at[:, cols(j)], weight.at[:, cols(j)], wsem.at[j])

    def keep_live_rows(ref, count):
        @pl.loop(count // GROUP, slots // GROUP)
        def _(g):
            rows = pl.ds(pl.multiple_of(CHUNK + g * GROUP, GROUP), GROUP)
            live = lax.broadcasted_iota(jnp.int32, (GROUP, 1), 0) + g * GROUP < count
            ref[rows, :] = jnp.where(live, ref[rows, :].astype(F32), 0.0).astype(BF16)

    def silu_of(linear, live):
        s = (0.5 * jnp.tanh(0.5 * linear) + 0.5) * live
        value = linear * s
        return value, s + value * (1.0 - s)

    def boundary(adj, targets):
        @pl.loop(0, width // FINE)
        def _(j):
            bnd_v[:, fine(j)] = lax.dot_general(
                adj, dagg_v[body, fine(j)], (((0,), (0,)), ((), ())), preferred_element_type=F32
            ).astype(BF16)
            start_all(targets(j))

    def first():
        out_chunk = tick + 1
        out_row = start + out_chunk * CHUNK
        out_valid = out_chunk < chunks
        got_chunk = tick - 1 - lag
        got_row = start + got_chunk * CHUNK
        got_valid = (got_chunk >= 0) & (got_chunk < chunks)

        def used(p):
            return out_valid & (offset_of(p) < out_row + CHUNK) & (end_of(p) > out_row)

        def load(p):
            return [
                pltpu.make_async_copy(ahat_ref.at[slot_of(p)], ahat.at[p % 2, body], asem.at[p % 2]),
                pltpu.make_async_copy(in_ref.at[slot_of(p)], x_v.at[p % 2], xsem.at[p % 2]),
            ]

        def completed(p):
            return got_valid & (end_of(p) > got_row) & (end_of(p) <= got_row + CHUNK)

        def load_back(p):
            return [
                pltpu.make_async_copy(ahat_ref.at[slot_of(p)], back_ahat, bsem.at[0]),
                pltpu.make_async_copy(dagg_ref.at[pl.ds(at(offset_of(p)), slots)], dagg_v.at[body], bsem.at[1]),
            ]

        load_g = pltpu.make_async_copy(got_ref.at[chunk], g_v, gsem.at[0])
        load_d = pltpu.make_async_copy(dfac_ref.at[pl.ds(at(got_row), CHUNK)], dback_v, gsem.at[1])
        first_used = first_of(used)
        first_completed = first_of(completed)

        @pl.when(first_used < clusters)
        def _():
            start_all(load(first_used))

        @pl.when(out_valid | got_valid)
        def _():
            start_all([load_weight(j) for j in range(tiles)])

        @pl.when(got_valid)
        def _():
            start_all([load_g, load_d])

        @pl.when(first_completed < clusters)
        def _():
            start_all(load_back(first_completed))

        there = pl.ds(at(out_row), CHUNK)
        outs = [
            pltpu.make_async_copy(act_v.at[chunk], next_ref, outsem.at[0]),
            pltpu.make_async_copy(agg_v.at[chunk], agg_ref.at[there], outsem.at[1]),
            pltpu.make_async_copy(dfac_v, dfac_ref.at[there], outsem.at[2]),
        ]

        def groups(act):
            @pl.loop(0, CHUNK // GROUP)
            def _(g):
                row = out_row + g * GROUP

                @pl.loop(0, clusters)
                def _(p):
                    @pl.when((row >= offset_of(p)) & (row < end_of(p)))
                    def _():
                        act(pltpu.make_async_copy(
                            act_v.at[pl.ds(pl.multiple_of(g * GROUP, GROUP), GROUP)],
                            act_ref.at[slot_of(p), pl.ds(at(row - offset_of(p)), GROUP)],
                            groupsem,
                        ))

        @pl.when(out_valid)
        def _():
            zero = jnp.zeros((CHUNK, slots), BF16)
            for i in range(2):
                ahat[i, pl.ds(0, CHUNK), :] = zero
                ahat[i, pl.ds(CHUNK + slots, CHUNK), :] = zero
            agg_v[chunk, :] = jnp.zeros((CHUNK, width), BF16)

            @pl.loop(0, clusters)
            def _(p):
                @pl.when(used(p))
                def _():
                    after = jnp.minimum(p + 1, clusters - 1)

                    @pl.when((p + 1 < clusters) & used(after))
                    def _():
                        start_all(load(after))

                    wait_all(load(p))
                    a = ahat[p % 2, pl.ds(at(CHUNK + out_row - offset_of(p)), CHUNK), :]
                    for j in range(tiles):
                        agg_v[chunk, cols(j)] += jnp.dot(a, x_v[p % 2, :, cols(j)], preferred_element_type=F32).astype(BF16)

            row_ids = lax.broadcasted_iota(jnp.int32, (CHUNK, 1), 0) + out_row
            live = jnp.zeros((CHUNK, 1), jnp.bool_)
            for p in range(clusters):
                live = live | ((row_ids >= offset_of(p)) & (row_ids < end_of(p)))
            live = live.astype(F32)
            outs[1].start()
            for j in range(tiles):
                load_weight(j).wait()
                linear = jnp.dot(agg_v[chunk, :], weight[:, cols(j)], preferred_element_type=F32) + bias_ref[:, cols(j)].astype(F32)
                value, factor = silu_of(linear, live)
                act_v[chunk, cols(j)] = value.astype(BF16)
                dfac_v[:, cols(j)] = factor
            outs[0].start()
            outs[2].start()
            groups(lambda copy: copy.start())

        @pl.when(got_valid & jnp.logical_not(out_valid))
        def _():
            wait_all([load_weight(j) for j in range(tiles)])

        @pl.when(got_valid)
        def _():
            wait_all([load_g, load_d])
            dlin_v[chunk, :] = (g_v[...].astype(F32) * dback_v[...]).astype(BF16)
            there = pl.ds(at(got_row), CHUNK)
            backs = [
                pltpu.make_async_copy(dlin_v.at[chunk], dlin_ref.at[there], gsem.at[0]),
                pltpu.make_async_copy(dpart_v, dagg_ref.at[there], gsem.at[1]),
            ]
            backs[0].start()
            for j in range(tiles):
                dpart_v[:, cols(j)] = lax.dot_general(
                    dlin_v[chunk, :], weight[cols(j), :], (((1,), (1,)), ((), ())), preferred_element_type=F32
                ).astype(BF16)

            @pl.loop(0, clusters)
            def _(p):
                @pl.when(completed(p))
                def _():
                    @pl.when(p != first_completed)
                    def _():
                        start_all(load_back(p))

                    wait_all(load_back(p))
                    dagg_v[pl.ds(at(CHUNK + got_row - offset_of(p)), CHUNK), :] = dpart_v[...]
                    keep_live_rows(dagg_v, count_of(p))

                    def targets(j):
                        return [pltpu.make_async_copy(bnd_v.at[:, fine(j)], bnd_ref.at[slot_of(p), :, fine(j)], bndsem.at[0, j])]

                    boundary(back_ahat[...], targets)
                    for j in range(width // FINE):
                        wait_all(targets(j))

            backs[1].start()
            wait_all(backs)

        @pl.when(out_valid)
        def _():
            wait_all(outs)
            groups(lambda copy: copy.wait())

    def second():
        got_chunk = tick - 1
        got_row = start + got_chunk * CHUNK
        got_valid = (got_chunk >= 0) & (got_chunk < chunks)
        out_chunk = tick + 1 - lag
        out_row = start + out_chunk * CHUNK
        out_valid = (out_chunk >= 0) & (tick < chunks)

        def ends_in(p, row):
            return (end_of(p) > row) & (end_of(p) <= row + CHUNK)

        def splits(p, row):
            after = jnp.where(p + 1 < clusters, end_of(jnp.minimum(p + 1, clusters - 1)), row + 2 * CHUNK)
            return (count_of(p) > STEP) & ends_in(p, row) & (after > row + CHUNK)

        def fresh(p):
            return got_valid & ends_in(p, got_row)

        def begun(p):
            return (got_chunk > 0) & splits(p, got_row - CHUNK)

        def task(p):
            return fresh(p) | begun(p)

        def load(p):
            return [
                pltpu.make_async_copy(recv_ref.at[pl.ds(at(offset_of(p)), slots)], rows_in.at[body], xsem.at[0]),
                pltpu.make_async_copy(ahat_ref.at[slot_of(p)], back_ahat, asem.at[0]),
            ]

        def load_begun(p):
            return [
                pltpu.make_async_copy(agg_ref.at[pl.ds(at(offset_of(p) + STEP), slots - STEP)], agg_v.at[pl.ds(STEP, slots - STEP)], xsem.at[0]),
                pltpu.make_async_copy(ahat_ref.at[slot_of(p)], back_ahat, asem.at[0]),
                pltpu.make_async_copy(dagg_ref.at[pl.ds(at(offset_of(p)), STEP)], dagg_v.at[pl.ds(CHUNK, STEP)], asem.at[1]),
            ]

        def load_g(p, r):
            here = pl.ds(pl.multiple_of(r * STEP, STEP), STEP)
            return pltpu.make_async_copy(in_ref.at[slot_of(p), here], x_v.at[0, here], xsem.at[1])

        def first_step(p):
            return jnp.where(fresh(p), 0, 1)

        def last_step(p):
            split = fresh(p) & splits(p, got_row) & (tick < chunks)
            return jnp.where(split, 1, (count_of(p) + STEP - 1) // STEP)

        def start_loads(p):
            @pl.when(fresh(p))
            def _():
                start_all(load(p))

            @pl.when(jnp.logical_not(fresh(p)))
            def _():
                start_all(load_begun(p))

            @pl.loop(first_step(p), last_step(p))
            def _(r):
                load_g(p, r).start()

        load_got = pltpu.make_async_copy(got_ref.at[chunk], g_v, gsem.at[0])
        keep_got = pltpu.make_async_copy(got_ref.at[chunk], recv_ref.at[pl.ds(at(got_row), CHUNK)], gsem.at[1])
        put_next = pltpu.make_async_copy(send_ref.at[pl.ds(at(out_row), CHUNK)], next_ref, nextsem)
        first_task = first_of(task)
        some = first_task < clusters
        new = out_valid & some & (offset_of(jnp.minimum(first_task, clusters - 1)) < out_row + CHUNK)

        @pl.when(some)
        def _():
            start_loads(first_task)
            start_all([load_weight(j) for j in range(tiles)])

        @pl.when(got_valid)
        def _():
            load_got.start()

        @pl.when(out_valid & jnp.logical_not(new))
        def _():
            put_next.start()

        @pl.when(got_valid)
        def _():
            load_got.wait()

        @pl.loop(0, clusters)
        def _(p):
            @pl.when(task(p))
            def _():
                offset, count, slot = offset_of(p), count_of(p), slot_of(p)
                steps = (count + STEP - 1) // STEP
                is_fresh = fresh(p)
                partial = is_fresh & splits(p, got_row) & (tick < chunks)

                @pl.when(p != first_task)
                def _():
                    start_loads(p)

                def keep_agg(r):
                    here = pl.ds(pl.multiple_of(r * STEP, STEP), STEP)
                    return pltpu.make_async_copy(agg_v.at[here], agg_ref.at[pl.ds(at(offset + r * STEP), STEP)], outsem.at[0])

                @pl.when(is_fresh)
                def _():
                    wait_all(load(p))
                    rows_in[pl.ds(at(CHUNK + got_row - offset), CHUNK), :] = g_v[...]
                    keep_live_rows(rows_in, count)

                    @pl.loop(0, tiles)
                    def _(j):
                        agg_v[:, cols(j)] = jnp.dot(back_ahat[...], rows_in[body, cols(j)], preferred_element_type=F32).astype(BF16)

                    @pl.loop(0, steps)
                    def _(r):
                        keep_agg(r).start()

                @pl.when(jnp.logical_not(is_fresh))
                def _():
                    wait_all(load_begun(p))

                @pl.loop(first_step(p), last_step(p))
                def _(r):
                    load_g(p, r).wait()

                def outs(r):
                    here = pl.ds(pl.multiple_of(r * STEP, STEP), STEP)
                    there = pl.ds(at(offset + r * STEP), STEP)
                    return [
                        pltpu.make_async_copy(act_v.at[here], act_ref.at[slot, here], outsem.at[1]),
                        pltpu.make_async_copy(dlin_v.at[here], dlin_ref.at[there], outsem.at[2]),
                    ]

                @pl.loop(first_step(p), last_step(p))
                def _(r):
                    here = pl.ds(pl.multiple_of(r * STEP, STEP), STEP)
                    live = (lax.broadcasted_iota(jnp.int32, (STEP, 1), 0) + r * STEP < count).astype(F32)

                    @pl.loop(0, tiles)
                    def _(j):
                        @pl.when((p == first_task) & (r == first_step(p)))
                        def _():
                            load_weight(j).wait()

                        linear = jnp.dot(agg_v[here, :], weight[:, cols(j)], preferred_element_type=F32) + bias_ref[:, cols(j)].astype(F32)
                        value, factor = silu_of(linear, live)
                        act_v[here, cols(j)] = value.astype(BF16)
                        dlin_v[here, cols(j)] = (x_v[0, here, cols(j)].astype(F32) * factor).astype(BF16)

                    start_all(outs(r))

                    @pl.loop(0, tiles)
                    def _(j):
                        dagg_v[pl.ds(pl.multiple_of(CHUNK + r * STEP, CHUNK), STEP), cols(j)] = lax.dot_general(
                            dlin_v[here, :], weight[cols(j), :], (((1,), (1,)), ((), ())), preferred_element_type=F32
                        ).astype(BF16)

                keep_dagg = pltpu.make_async_copy(dagg_v.at[pl.ds(CHUNK, STEP)], dagg_ref.at[pl.ds(at(offset), STEP)], asem.at[1])

                @pl.when(partial)
                def _():
                    keep_dagg.start()
                    keep_dagg.wait()

                @pl.when(jnp.logical_not(partial))
                def _():
                    @pl.loop(steps, slots // STEP)
                    def _(r):
                        dagg_v[pl.ds(pl.multiple_of(CHUNK + r * STEP, CHUNK), STEP), :] = jnp.zeros((STEP, width), BF16)

                    def targets(j):
                        return [
                            pltpu.make_async_copy(bnd_v.at[:, fine(j)], send_ref.at[pl.ds(at(offset), slots), fine(j)], bndsem.at[0, j]),
                            pltpu.make_async_copy(bnd_v.at[:, fine(j)], bnd_ref.at[slot, :, fine(j)], bndsem.at[1, j]),
                        ]

                    boundary(back_ahat[...], targets)
                    for j in range(width // FINE):
                        wait_all(targets(j))

                @pl.loop(first_step(p), last_step(p))
                def _(r):
                    wait_all(outs(r))

                @pl.when(is_fresh)
                def _():
                    @pl.loop(0, steps)
                    def _(r):
                        keep_agg(r).wait()

        @pl.when(got_valid)
        def _():
            keep_got.start()

        @pl.when(new)
        def _():
            put_next.start()

        @pl.when(got_valid)
        def _():
            keep_got.wait()

        @pl.when(out_valid)
        def _():
            put_next.wait()

    pl.when(first_section)(first)
    pl.when(jnp.logical_not(first_section))(second)


def run_tick(tick, plan, section_rows, ahat, weight, bias, got, state, packed):
    clusters, slots, width = section_rows.shape
    tiles = width // TILE
    state_shapes = tuple(jax.ShapeDtypeStruct(s.shape, s.dtype) for s in state)
    cluster = pltpu.VMEM((slots, width), BF16)
    roomy = pltpu.VMEM((slots + 2 * CHUNK, width), BF16)
    chunk = pltpu.VMEM((CHUNK, width), BF16)
    chunk32 = pltpu.VMEM((CHUNK, width), F32)
    dma = pltpu.SemaphoreType.DMA
    outs = pl.pallas_call(
        functools.partial(tick_kernel, clusters, slots, width, packed),
        out_shape=(jax.ShapeDtypeStruct((CHUNK, width), BF16),) + state_shapes,
        in_specs=[SMEM, SMEM, ANY, ANY, ANY, VMEM, ANY] + [HBM] * 8,
        out_specs=(ANY,) + (HBM,) * 8,
        input_output_aliases={7 + i: 1 + i for i in range(8)},
        scratch_shapes=[
            pltpu.VMEM((width, width), BF16),
            pltpu.VMEM((2, slots + 2 * CHUNK, slots), BF16),
            pltpu.VMEM((slots, slots), BF16),
            roomy,
            pltpu.VMEM((2, slots, width), BF16),
            chunk, cluster, cluster, cluster, roomy, chunk, cluster, chunk32, chunk32,
            dma((tiles,)), dma((2,)), dma((2,)), dma((2,)), dma((2,)), dma((3,)), dma((2, width // FINE)), dma, dma,
        ],
        compiler_params=pltpu.CompilerParams(vmem_limit_bytes=57 << 20, has_side_effects=True),
        cost_estimate=pl.CostEstimate(flops=6 * CHUNK * width * width, bytes_accessed=2 * width * width, transcendentals=0),
    )(tick, plan, section_rows, ahat, weight, bias, got, *state)
    return outs[0], outs[1:]


def tracks_of(n, rows):
    weights = [2**q for q in range(n.bit_length() - 1)]
    part = rows // 4
    if len(weights) < 3 or part // n < 16:
        return [(0, rows, weights)]
    return [(0, rows - part, weights), (rows - part, part, [weights[0], weights[2], weights[1]] + weights[3:])]


def finish_kernel(
    n, block, halves, rows, back,
    agg_ref, dlin_ref, dfac_ref, send_ref, last_ref, weight_ref, out_ref, db_ref, dagg_ref,
    agg, dlin, acc, sbuf, rbuf, res, got, dfac, dsend, drecv, dsum, dacc, dagg_v, last_v,
    lsem, wsem, bsem, osem, ssem, rsem, gssem, grsem, dssem, drsem, xssem, xrsem,
):
    width = dlin.shape[1]
    slots, rows_out = acc.shape[0], acc.shape[1]
    nb = res.shape[0]
    column_blocks = nb // halves
    section = lax.axis_index("section")
    me = lax.axis_index("dp")
    tracks = tracks_of(n, rows_out)
    depth = len(tracks[0][2])
    late = pl.ds(rows - back, back)
    drained = pl.ds(rows - back + CHUNK, back - CHUNK)
    hops = [(s, m) for s in range(depth) for m in range(len(tracks))]

    def bit(m, s):
        return (me // tracks[m][2][s]) % 2

    def partner(s, m):
        return (section, me + (1 - 2 * bit(m, s)) * tracks[m][2][s])

    across = (1 - section, me)
    barrier = pltpu.get_barrier_semaphore()
    for s in range(depth):
        pl.semaphore_signal(barrier, inc=1, device_id=partner(s, 0), device_id_type=MESH)
    pl.semaphore_signal(barrier, inc=1, device_id=across, device_id_type=MESH)
    load_dlin = pltpu.make_async_copy(dlin_ref.at[pl.ds(0, rows)], dlin, lsem.at[0])
    load_agg = pltpu.make_async_copy(agg_ref.at[pl.ds(0, rows)], agg, lsem.at[1])
    load_weight = pltpu.make_async_copy(weight_ref, agg, wsem)
    load_dlin.start()
    load_agg.start()
    pl.semaphore_wait(barrier, depth + 1)

    def columns(c):
        return pl.ds(pl.multiple_of(c * block, block), block)

    def drain(c):
        return pltpu.make_async_remote_copy(
            src_ref=send_ref.at[drained, columns(c)], dst_ref=got.at[c], send_sem=xssem.at[c], recv_sem=xrsem.at[c],
            device_id=across, device_id_type=MESH)

    def load_back(c):
        return [
            pltpu.make_async_copy(dfac_ref.at[late, columns(c)], dfac.at[c % 2], bsem.at[c % 2, 0]),
            pltpu.make_async_copy(last_ref.at[:, columns(c)], last_v.at[c % 2], bsem.at[c % 2, 1]),
        ]

    @pl.when(section == 1)
    def _():
        for c in range(min(2, column_blocks)):
            drain(c).start()

    @pl.when(section == 0)
    def _():
        for copy in load_back(0):
            copy.start()

    def size(m, s):
        return tracks[m][1] >> s

    def piece(m, s):
        row = tracks[m][0]
        for q in range(s):
            row = row + bit(m, q) * size(m, q + 1)
        return row

    def other(m, s):
        return piece(m, s) + (1 - bit(m, s)) * size(m, s + 1)

    def rows_at(row, m, s):
        return pl.ds(pl.multiple_of(row, 16), size(m, s + 1))

    def staged(m, s):
        return pl.ds(tracks[m][0] + tracks[m][1] - size(m, s), size(m, s + 1))

    def rs(b, s, m):
        return pltpu.make_async_remote_copy(
            src_ref=sbuf.at[b, staged(m, s)], dst_ref=rbuf.at[b, staged(m, s)],
            send_sem=ssem.at[b, s, m], recv_sem=rsem.at[b, s, m], device_id=partner(s, m), device_id_type=MESH)

    def rs_start(b, s):
        for m in range(len(tracks)):
            sbuf[b, staged(m, s), :] = acc[b % slots, rows_at(other(m, s), m, s), :].astype(BF16)
            rs(b, s, m).start()

    def rs_end(b, s):
        for m in range(len(tracks)):
            here = rows_at(piece(m, s + 1), m, s)
            rs(b, s, m).wait_recv()
            total = acc[b % slots, here, :] + rbuf[b, staged(m, s), :].astype(F32)
            if s + 1 < depth:
                acc[b % slots, here, :] = total
            else:
                res[b, here, :] = total.astype(BF16)

    def ag(b, s, m, row):
        here = res.at[b, rows_at(row, m, s)]
        return pltpu.make_async_remote_copy(
            src_ref=here, dst_ref=here, send_sem=gssem.at[b, s, m], recv_sem=grsem.at[b, s, m],
            device_id=partner(s, m), device_id_type=MESH)

    def ag_start(b, s):
        for m in range(len(tracks)):
            ag(b, s, m, piece(m, s + 1)).start()

    def ag_end(b, s):
        for m in range(len(tracks)):
            ag(b, s, m, other(m, s)).wait_recv()

    def out(b):
        return pltpu.make_async_copy(res.at[b], out_ref.at[b], osem.at[b])

    def product(b):
        c = b // halves

        @pl.when(b % halves == 0)
        def _():
            @pl.when(section == 1)
            def _():
                drain(c).wait_send()

                @pl.when(c + 2 < column_blocks)
                def _():
                    drain(c + 2).start()

            @pl.when(section == 0)
            def _():
                for copy in load_back(c):
                    copy.wait()

                @pl.when(c + 1 < column_blocks)
                def _():
                    for copy in load_back(c + 1):
                        copy.start()

                last = last_v[c % 2]
                factor = dfac[c % 2, pl.ds(0, CHUNK)]
                value = jnp.where(factor == 0.0, 0.0, last.astype(F32) * factor)
                dlin[pl.ds(rows - back, CHUNK), columns(c)] = value.astype(BF16)
                drain(c).wait_recv()
                dlin[drained, columns(c)] = (got[c].astype(F32) * dfac[c % 2, pl.ds(CHUNK, back - CHUNK)]).astype(BF16)

            @pl.loop(0, rows // 256)
            def _(i):
                some = dlin[pl.ds(pl.multiple_of(i * 256, 256), 256), columns(c)].astype(F32)
                dacc[:, columns(c)] += jnp.sum(some.reshape(32, 8, block), axis=0)


        d = dlin[:, columns(c)]
        part = min(rows_out, 512 if slots < nb else 256)

        @pl.loop(0, rows_out // part)
        def _(i):
            r = pl.ds(pl.multiple_of(i * part, part), part)
            a = agg[:, pl.ds(pl.multiple_of((b % halves) * rows_out + i * part, part), part)]
            acc[b % slots, r, :] = lax.dot_general(a, d, (((0,), (0,)), ((), ())), preferred_element_type=F32)

    def stage(b, k):
        if k == 0:
            product(b)
            rs_start(b, 0)
        elif k < depth:
            rs_end(b, k - 1)
            rs_start(b, k)
        elif k == depth:
            rs_end(b, k - 1)
            ag_start(b, depth - 1)
        else:
            s = 2 * depth - k
            ag_end(b, s)
            if s > 0:
                ag_start(b, s - 1)
            else:
                out(b).start()

    bits = dsend.shape[0]

    def db(q):
        to = (section, me + (1 - 2 * ((me // 2**q) % 2)) * 2**q)
        return pltpu.make_async_remote_copy(
            src_ref=dsend.at[q], dst_ref=drecv.at[q], send_sem=dssem.at[q], recv_sem=drsem.at[q],
            device_id=to, device_id_type=MESH)

    def db_step(q):
        if q == 0:
            whole = jnp.sum(dacc[...], axis=0, keepdims=True)
            for i in range(8):
                dsum[i:i + 1, :] = whole[:, i * (width // 8):(i + 1) * (width // 8)]
        else:
            db(q - 1).wait_recv()
            dsum[...] += drecv[q - 1]
        if q < bits:
            dsend[q] = dsum[...]
            db(q).start()

    parts = back // dagg_v.shape[0]

    def dagg_part(i):
        size = dagg_v.shape[0]
        first = pl.multiple_of(rows - back + i * size, 32)

        @pl.loop(0, width // 512)
        def _(j):
            c = pl.ds(pl.multiple_of(j * 512, 512), 512)
            dagg_v[:, c] = lax.dot_general(
                dlin[pl.ds(first, size), :], agg[c, :], (((1,), (1,)), ((), ())), preferred_element_type=F32
            ).astype(BF16)

        copy = pltpu.make_async_copy(dagg_v, dagg_ref.at[pl.ds(pl.multiple_of(i * size, 32), size)], lsem.at[0])
        copy.start()
        copy.wait()

    dacc[...] = jnp.zeros_like(dacc)
    load_dlin.wait()
    load_agg.wait()
    stages = 2 * depth + 1

    @pl.loop(0, nb + stages - 1)
    def _(step):
        for k in reversed(range(stages)):
            b = step - k

            @pl.when((b >= 0) & (b < nb))
            def _():
                stage(b, k)

        @pl.when((step == nb - 1) & (section == 0))
        def _():
            load_weight.start()

        for q in range(min(bits + 1, stages - 1)):
            @pl.when(step == nb + q)
            def _():
                db_step(q)

        @pl.when((step == nb) & (section == 0))
        def _():
            load_weight.wait()

        @pl.when((step >= nb) & (step < nb + parts) & (section == 0))
        def _():
            dagg_part(step - nb)

    for q in range(min(bits + 1, stages - 1), bits + 1):
        db_step(q)
    db_ref[...] = dsum[...]

    @pl.loop(0, nb)
    def _(b):
        for s, m in hops:
            rs(b, s, m).wait_send()
            ag(b, s, m, piece(m, s + 1)).wait_send()
        out(b).wait()

    for q in range(bits):
        db(q).wait_send()


def finish(n, agg, dlin, dfac, send, last, weight, rows, back):
    width = weight.shape[1]
    bits = n.bit_length() - 1
    block = 256
    halves = 2 if weight.shape[0] // n >= 128 else 1
    rows_out = weight.shape[0] // halves
    column_blocks = width // block
    nb = column_blocks * halves
    slots = min(nb, bits + 1)
    tracks = len(tracks_of(n, rows_out))
    dma = pltpu.SemaphoreType.DMA
    return pl.pallas_call(
        functools.partial(finish_kernel, n, block, halves, rows, back),
        out_shape=(
            jax.ShapeDtypeStruct((nb, rows_out, block), BF16),
            jax.ShapeDtypeStruct((8, width // 8), F32),
            jax.ShapeDtypeStruct((back, width), BF16),
        ),
        in_specs=[ANY] * 6,
        out_specs=(ANY, VMEM, ANY),
        scratch_shapes=[
            pltpu.VMEM((rows, weight.shape[0]), BF16),
            pltpu.VMEM((rows, width), BF16),
            pltpu.VMEM((slots, rows_out, block), F32),
            pltpu.VMEM((nb, rows_out, block), BF16),
            pltpu.VMEM((nb, rows_out, block), BF16),
            pltpu.VMEM((nb, rows_out, block), BF16),
            pltpu.VMEM((column_blocks, back - CHUNK, block), BF16),
            pltpu.VMEM((2, back, block), F32),
            pltpu.VMEM((bits, 8, width // 8), F32),
            pltpu.VMEM((bits, 8, width // 8), F32),
            pltpu.VMEM((8, width // 8), F32),
            pltpu.VMEM((8, width), F32),
            pltpu.VMEM((back // 4, width), BF16),
            pltpu.VMEM((2, CHUNK, block), BF16),
            dma((2,)), dma, dma((2, 2)), dma((nb,)),
            dma((nb, bits, tracks)), dma((nb, bits, tracks)), dma((nb, bits, tracks)), dma((nb, bits, tracks)),
            dma((bits,)), dma((bits,)), dma((column_blocks,)), dma((column_blocks,)),
        ],
        compiler_params=pltpu.CompilerParams(collective_id=1, has_side_effects=True, vmem_limit_bytes=63 << 20),
        cost_estimate=pl.CostEstimate(flops=2 * rows * weight.shape[0] * width, bytes_accessed=rows * width * 8, transcendentals=0),
    )(agg, dlin, dfac, send, last, weight)


def closing_kernel(
    clusters, slots, packed, back, plan_ref, blocks_ref, sums_ref, ahat_ref, dagg_ref, late_ref, bnd_i,
    grad_ref, bias_ref, bnd_ref, ahat, source, bnd_v, sem, asem, osem,
):
    step = pl.program_id(0)
    first_section = lax.axis_index("section") == 0
    low = packed - back - slots
    loads = [
        pltpu.make_async_copy(dagg_ref.at[pl.ds(low, slots)], source.at[pl.ds(0, slots)], sem.at[0]),
        pltpu.make_async_copy(late_ref, source.at[pl.ds(slots, back)], sem.at[1]),
    ]

    def load_ahat(p):
        return pltpu.make_async_copy(ahat_ref.at[plan_ref[SLOT, p]], ahat.at[p], asem.at[p])

    def late(p):
        return first_section & (plan_ref[OFFSET, p] + plan_ref[COUNT, p] > packed - back)

    def store(p):
        return pltpu.make_async_copy(bnd_v.at[p % 2], bnd_ref.at[plan_ref[SLOT, p]], osem.at[p % 2])

    @pl.when(step == 0)
    def _():
        part = sums_ref.shape[1]
        for i in range(8):
            bias_ref[:, i * part:(i + 1) * part] = sums_ref[i:i + 1, :]

    @pl.when(first_section & (step == 0))
    def _():
        for load in loads:
            load.start()
        for p in range(clusters):
            @pl.when(late(p))
            def _():
                load_ahat(p).start()
        source[pl.ds(slots + back, slots), :] = jnp.zeros((slots, source.shape[1]), BF16)

    part = blocks_ref.shape[1]
    for i in range(blocks_ref.shape[0]):
        grad_ref[i * part:(i + 1) * part, :] = blocks_ref[i].astype(F32)

    @pl.when(first_section & (step == 1))
    def _():
        for load in loads:
            load.wait()

    half = source.shape[1] // 2
    for p in range(clusters):
        @pl.when((step == 2 * p + 1) & late(p))
        def _():
            load_ahat(p).wait()

        if p >= 2:
            @pl.when((step == 2 * p + 1) & late(p - 2))
            def _():
                store(p - 2).wait()

        @pl.when(((step == 2 * p + 1) | (step == 2 * p + 2)) & late(p))
        def _():
            rows = pl.ds(pl.multiple_of(plan_ref[OFFSET, p] - low, GROUP), slots)
            cols = pl.ds(pl.multiple_of((step - 2 * p - 1) * half, half), half)
            bnd_v[p % 2, :, cols] = lax.dot_general(
                ahat[p], source[rows, cols], (((0,), (0,)), ((), ())), preferred_element_type=F32
            ).astype(BF16)

        @pl.when((step == 2 * p + 2) & late(p))
        def _():
            store(p).start()

    for p in range(max(clusters - 2, 0), clusters):
        @pl.when((step == pl.num_programs(0) - 1) & late(p))
        def _():
            store(p).wait()


def closing(plan, blocks, sums, ahat, dagg, late, bnd, packed):
    nb, rows, block = blocks.shape
    clusters, slots, width = bnd.shape
    halves = nb * block // width
    column_blocks = nb // halves
    back = late.shape[0]
    steps = max(column_blocks, 2 * clusters + 1)
    return pl.pallas_call(
        functools.partial(closing_kernel, clusters, slots, packed, back),
        grid=(steps,),
        out_shape=(
            jax.ShapeDtypeStruct((rows * halves, width), F32),
            jax.ShapeDtypeStruct((1, width), F32),
            jax.ShapeDtypeStruct(bnd.shape, BF16),
        ),
        in_specs=[SMEM, pl.BlockSpec((halves, rows, block), lambda b: (jnp.minimum(b, column_blocks - 1), 0, 0)), VMEM] + [ANY] * 4,
        out_specs=(
            pl.BlockSpec((rows * halves, block), lambda b: (0, jnp.minimum(b, column_blocks - 1))),
            pl.BlockSpec((1, width), lambda b: (0, 0)),
            ANY,
        ),
        input_output_aliases={6: 2},
        scratch_shapes=[
            pltpu.VMEM((clusters, slots, slots), BF16),
            pltpu.VMEM((2 * slots + back, width), BF16),
            pltpu.VMEM((2, slots, width), BF16),
            pltpu.SemaphoreType.DMA((2,)),
            pltpu.SemaphoreType.DMA((clusters,)),
            pltpu.SemaphoreType.DMA((2,)),
        ],
        compiler_params=pltpu.CompilerParams(vmem_limit_bytes=60 << 20, has_side_effects=True),
    )(plan, blocks, sums, ahat, dagg, late, bnd)


def per_device(section_inputs, neighbours, counts, weight, bias):
    section_rows = section_inputs[0]
    weight_one = weight[0]
    clusters, slots, width = section_rows.shape
    packed = clusters * slots
    back = lag_of(slots) * CHUNK
    ahat, plan, *state = prepare(counts, jnp.swapaxes(neighbours, 1, 2), width, packed, slots)
    state = tuple(state)
    swap = [(0, 1), (1, 0)]

    def step(tick, got, state):
        return run_tick(tick, plan, section_rows, ahat, weight_one, bias, got, state, packed)

    first = jnp.full((1,), -1, jnp.int32)
    send, state = step(first, weight_one, state)
    send, last_plan = lax.optimization_barrier((send, plan))
    chunks = last_plan[REST, CHUNKS]

    def more(carry):
        return carry[0][0] <= chunks

    def body(carry):
        tick, send, got, state = carry
        arrives = lax.ppermute(send, "section", swap)
        send, state = step(tick, got, state)
        return tick + 1, send, arrives, state

    tick, send, got, state = lax.while_loop(more, body, (first + 1, send, send, state))
    agg, dlin, dfac, to_send, recv, dagg, act, bnd = state
    blocks, sums, late = finish(lax.axis_size("dp"), agg, dlin, dfac, to_send, got, weight_one, packed, back)
    grad_weight, grad_bias, bnd = closing(plan, blocks, sums, ahat, dagg, late, bnd, packed)
    return act[None], bnd[None], grad_weight[None], grad_bias


def solution(mesh):
    return jax.shard_map(
        per_device,
        mesh=mesh,
        in_specs=(
            P("section", "dp", None, None),
            P("dp", None, None),
            P("dp"),
            P("section", None, None),
            P("section", None),
        ),
        out_specs=(
            P("section", "dp", None, None),
            P("section", "dp", None, None),
            P("section", None, None),
            P("section", None),
        ),
        check_vma=False,
    )
```

```python
import functools

import jax
import jax.numpy as jnp
from jax import lax
from jax.experimental import pallas as pl
from jax.experimental.pallas import tpu as pltpu
from jax.sharding import PartitionSpec as P

MESH = pl.DeviceIdType.MESH
ANY = pl.BlockSpec(memory_space=pl.ANY)
HBM = pl.BlockSpec(memory_space=pltpu.MemorySpace.HBM)
SMEM = pl.BlockSpec(memory_space=pltpu.SMEM)
VMEM = pl.BlockSpec(memory_space=pltpu.VMEM)
F32, BF16 = jnp.float32, jnp.bfloat16

CHUNK = 128
STEP = 256
GROUP = 16
TILE = 1024
FINE = 512
COUNT, OFFSET, SLOT, REST = 0, 1, 2, 3
CHUNKS = 0


def lag_of(slots):
    return (slots - 1 + CHUNK - 1) // CHUNK + 3


def up(x, by):
    return (x + by - 1) // by * by


def prepare_kernel(
    clusters, slots, packed, counts_ref, neighbours_ref,
    ahat_ref, plan_ref, agg_ref, dlin_ref, dfac_ref, send_ref, recv_ref, dagg_ref, act_ref, bnd_ref,
    zeros, zeros32, targets, sem,
):
    c = pl.program_id(0)
    counts = [counts_ref[i] for i in range(clusters)]
    total = sum(up(n, GROUP) for n in counts)
    chunks = (total + CHUNK - 1) // CHUNK
    start = packed - chunks * CHUNK
    front = (start + CHUNK) // CHUNK
    backlog = packed // CHUNK - lag_of(slots)

    def each(act):
        for ref, first in ((agg_ref, 0), (dlin_ref, 0), (send_ref, jnp.minimum(front - 1, backlog))):
            @pl.loop(first, front)
            def _(i):
                act(pltpu.make_async_copy(zeros, ref.at[pl.ds(pl.multiple_of(i * CHUNK, CHUNK), CHUNK)], sem))

        @pl.loop(backlog, front)
        def _(i):
            act(pltpu.make_async_copy(zeros32, dfac_ref.at[pl.ds(pl.multiple_of(i * CHUNK, CHUNK), CHUNK)], sem))

        for i in range(clusters):
            whole = (counts[i] + CHUNK - 1) // CHUNK

            @pl.loop((counts[i] + GROUP - 1) // GROUP, whole * (CHUNK // GROUP))
            def _(g):
                rows = pl.ds(pl.multiple_of(g * GROUP, GROUP), GROUP)
                act(pltpu.make_async_copy(zeros.at[pl.ds(0, GROUP)], act_ref.at[i, rows], sem))

            @pl.loop(whole, slots // CHUNK)
            def _(g):
                act(pltpu.make_async_copy(zeros, act_ref.at[i, pl.ds(pl.multiple_of(g * CHUNK, CHUNK), CHUNK)], sem))

    @pl.when(c == 0)
    def _():
        zeros[...] = jnp.zeros_like(zeros)
        zeros32[...] = jnp.zeros_like(zeros32)
        each(lambda copy: copy.start())
        for i in range(clusters):
            rank = 0
            for j in range(clusters):
                ahead = counts[j] >= counts[i] if j < i else counts[j] > counts[i]
                rank = rank + (ahead.astype(jnp.int32) if j != i else 0)
            plan_ref[COUNT, rank] = counts[i]
            plan_ref[SLOT, rank] = i
        offset = packed - total
        for i in range(clusters):
            plan_ref[OFFSET, i] = offset
            offset = offset + up(plan_ref[COUNT, i], GROUP)
        plan_ref[REST, CHUNKS] = chunks

    count = counts_ref[c]
    slots_each = neighbours_ref.shape[1]
    neighbours = neighbours_ref[0].astype(F32)
    size = count.astype(F32)
    targets[:, 0:slots_each] = jnp.transpose(neighbours - jnp.floor((neighbours + 0.5) / size) * size)
    group = 64
    groups = (count + group - 1) // group

    @pl.loop(0, groups)
    def _(g):
        rows = pl.ds(pl.multiple_of(g * group, group), group)
        here = targets[rows, :].astype(jnp.int32)
        columns = lax.broadcasted_iota(jnp.int32, (group, slots), 1)
        row_ids = lax.broadcasted_iota(jnp.int32, (group, slots), 0) + g * group
        adjacency = jnp.zeros((group, slots), F32)
        for k in range(slots_each):
            adjacency = adjacency + jnp.where(here[:, k:k + 1] == columns, 1.0, 0.0)
        a = jnp.where(row_ids == columns, 2.0 * adjacency + 2.0, adjacency) / (1.0 + slots_each)
        ahat_ref[0, rows, :] = jnp.where(row_ids < count, a, 0.0).astype(BF16)

    @pl.loop(groups, slots // group)
    def _(g):
        ahat_ref[0, pl.ds(pl.multiple_of(g * group, group), group), :] = jnp.zeros((group, slots), BF16)

    @pl.when(c == clusters - 1)
    def _():
        each(lambda copy: copy.wait())


def prepare(counts, neighbours, width, packed, margin):
    clusters, slots_each, slots = neighbours.shape
    rows = jax.ShapeDtypeStruct((packed + margin, width), BF16)
    rows32 = jax.ShapeDtypeStruct((packed, width), F32)
    whole = jax.ShapeDtypeStruct((clusters, slots, width), BF16)
    return pl.pallas_call(
        functools.partial(prepare_kernel, clusters, slots, packed),
        grid=(clusters,),
        out_shape=(
            jax.ShapeDtypeStruct((clusters, slots, slots), BF16),
            jax.ShapeDtypeStruct((4, max(clusters, 4)), jnp.int32),
            rows, rows, rows32, rows, rows, rows, whole, whole,
        ),
        in_specs=[SMEM, pl.BlockSpec((1, slots_each, slots), lambda c: (c, 0, 0))],
        out_specs=(pl.BlockSpec((1, slots, slots), lambda c: (c, 0, 0)), SMEM) + (HBM,) * 8,
        scratch_shapes=[pltpu.VMEM((CHUNK, width), BF16), pltpu.VMEM((CHUNK, width), F32), pltpu.VMEM((slots, 128), F32), pltpu.SemaphoreType.DMA],
        compiler_params=pltpu.CompilerParams(vmem_limit_bytes=60 << 20),
    )(counts, neighbours)


def tick_kernel(
    clusters, slots, width, packed,
    tick_ref, plan_ref, in_ref, ahat_ref, weight_ref, bias_ref, got_ref,
    agg_i, dlin_i, dfac_i, send_i, recv_i, dagg_i, act_i, bnd_i,
    next_ref, agg_ref, dlin_ref, dfac_ref, send_ref, recv_ref, dagg_ref, act_ref, bnd_ref,
    weight, ahat, back_ahat, rows_in, x_v, g_v, agg_v, act_v, dlin_v, dagg_v, dpart_v, bnd_v, dfac_v, dback_v,
    wsem, asem, xsem, bsem, gsem, outsem, bndsem, groupsem, nextsem,
):
    first_section = lax.axis_index("section") == 0
    tick = tick_ref[0]
    chunks = plan_ref[REST, CHUNKS]
    lag = lag_of(slots)
    start = packed - chunks * CHUNK
    tiles = width // TILE
    chunk = pl.ds(0, CHUNK)
    body = pl.ds(CHUNK, slots)

    def at(i):
        return pl.multiple_of(i, GROUP)

    def cols(j):
        return pl.ds(pl.multiple_of(j * TILE, TILE), TILE)

    def fine(j):
        return pl.ds(pl.multiple_of(j * FINE, FINE), FINE)

    def count_of(p):
        return plan_ref[COUNT, p]

    def offset_of(p):
        return plan_ref[OFFSET, p]

    def slot_of(p):
        return plan_ref[SLOT, p]

    def end_of(p):
        return offset_of(p) + count_of(p)

    def first_of(test):
        found = clusters
        for p in reversed(range(clusters)):
            found = jnp.where(test(p), p, found)
        return found

    def start_all(copies):
        for copy in copies:
            copy.start()

    def wait_all(copies):
        for copy in copies:
            copy.wait()

    def load_weight(j):
        return pltpu.make_async_copy(weight_ref.at[:, cols(j)], weight.at[:, cols(j)], wsem.at[j])

    def keep_live_rows(ref, count):
        @pl.loop(count // GROUP, slots // GROUP)
        def _(g):
            rows = pl.ds(pl.multiple_of(CHUNK + g * GROUP, GROUP), GROUP)
            live = lax.broadcasted_iota(jnp.int32, (GROUP, 1), 0) + g * GROUP < count
            ref[rows, :] = jnp.where(live, ref[rows, :].astype(F32), 0.0).astype(BF16)

    def silu_of(linear, live):
        s = (0.5 * jnp.tanh(0.5 * linear) + 0.5) * live
        value = linear * s
        return value, s + value * (1.0 - s)

    def boundary(adj, targets):
        @pl.loop(0, width // FINE)
        def _(j):
            bnd_v[:, fine(j)] = lax.dot_general(
                adj, dagg_v[body, fine(j)], (((0,), (0,)), ((), ())), preferred_element_type=F32
            ).astype(BF16)
            start_all(targets(j))

    def first():
        out_chunk = tick + 1
        out_row = start + out_chunk * CHUNK
        out_valid = out_chunk < chunks
        got_chunk = tick - 1 - lag
        got_row = start + got_chunk * CHUNK
        got_valid = (got_chunk >= 0) & (got_chunk < chunks)

        def used(p):
            return out_valid & (offset_of(p) < out_row + CHUNK) & (end_of(p) > out_row)

        def load(p):
            return [
                pltpu.make_async_copy(ahat_ref.at[slot_of(p)], ahat.at[p % 2, body], asem.at[p % 2]),
                pltpu.make_async_copy(in_ref.at[slot_of(p)], x_v.at[p % 2], xsem.at[p % 2]),
            ]

        def completed(p):
            return got_valid & (end_of(p) > got_row) & (end_of(p) <= got_row + CHUNK)

        def load_back(p):
            return [
                pltpu.make_async_copy(ahat_ref.at[slot_of(p)], back_ahat, bsem.at[0]),
                pltpu.make_async_copy(dagg_ref.at[pl.ds(at(offset_of(p)), slots)], dagg_v.at[body], bsem.at[1]),
            ]

        load_g = pltpu.make_async_copy(got_ref.at[chunk], g_v, gsem.at[0])
        load_d = pltpu.make_async_copy(dfac_ref.at[pl.ds(at(got_row), CHUNK)], dback_v, gsem.at[1])
        first_used = first_of(used)
        first_completed = first_of(completed)

        @pl.when(first_used < clusters)
        def _():
            start_all(load(first_used))

        @pl.when(out_valid | got_valid)
        def _():
            start_all([load_weight(j) for j in range(tiles)])

        @pl.when(got_valid)
        def _():
            start_all([load_g, load_d])

        @pl.when(first_completed < clusters)
        def _():
            start_all(load_back(first_completed))

        there = pl.ds(at(out_row), CHUNK)
        outs = [
            pltpu.make_async_copy(act_v.at[chunk], next_ref, outsem.at[0]),
            pltpu.make_async_copy(agg_v.at[chunk], agg_ref.at[there], outsem.at[1]),
            pltpu.make_async_copy(dfac_v, dfac_ref.at[there], outsem.at[2]),
        ]

        def groups(act):
            @pl.loop(0, CHUNK // GROUP)
            def _(g):
                row = out_row + g * GROUP
                p = -1
                for q in range(clusters):
                    p = p + (row >= offset_of(q)).astype(jnp.int32)
                here = jnp.maximum(p, 0)

                @pl.when((p >= 0) & (row < end_of(here)))
                def _():
                    act(pltpu.make_async_copy(
                        act_v.at[pl.ds(pl.multiple_of(g * GROUP, GROUP), GROUP)],
                        act_ref.at[slot_of(here), pl.ds(at(row - offset_of(here)), GROUP)],
                        groupsem,
                    ))

        @pl.when(out_valid)
        def _():
            zero = jnp.zeros((CHUNK, slots), BF16)
            for i in range(2):
                ahat[i, pl.ds(0, CHUNK), :] = zero
                ahat[i, pl.ds(CHUNK + slots, CHUNK), :] = zero
            agg_v[chunk, :] = jnp.zeros((CHUNK, width), BF16)

            @pl.loop(0, clusters)
            def _(p):
                @pl.when(used(p))
                def _():
                    after = jnp.minimum(p + 1, clusters - 1)

                    @pl.when((p + 1 < clusters) & used(after))
                    def _():
                        start_all(load(after))

                    wait_all(load(p))
                    a = ahat[p % 2, pl.ds(at(CHUNK + out_row - offset_of(p)), CHUNK), :]
                    for j in range(tiles):
                        agg_v[chunk, cols(j)] += jnp.dot(a, x_v[p % 2, :, cols(j)], preferred_element_type=F32).astype(BF16)

            row_ids = lax.broadcasted_iota(jnp.int32, (CHUNK, 1), 0) + out_row
            live = jnp.zeros((CHUNK, 1), jnp.bool_)
            for p in range(clusters):
                live = live | ((row_ids >= offset_of(p)) & (row_ids < end_of(p)))
            live = live.astype(F32)
            outs[1].start()
            for j in range(tiles):
                load_weight(j).wait()
                linear = jnp.dot(agg_v[chunk, :], weight[:, cols(j)], preferred_element_type=F32) + bias_ref[:, cols(j)].astype(F32)
                value, factor = silu_of(linear, live)
                act_v[chunk, cols(j)] = value.astype(BF16)
                dfac_v[:, cols(j)] = factor
            outs[0].start()
            outs[2].start()
            groups(lambda copy: copy.start())

        @pl.when(got_valid & jnp.logical_not(out_valid))
        def _():
            wait_all([load_weight(j) for j in range(tiles)])

        @pl.when(got_valid)
        def _():
            wait_all([load_g, load_d])
            dlin_v[chunk, :] = (g_v[...].astype(F32) * dback_v[...]).astype(BF16)
            there = pl.ds(at(got_row), CHUNK)
            backs = [
                pltpu.make_async_copy(dlin_v.at[chunk], dlin_ref.at[there], gsem.at[0]),
                pltpu.make_async_copy(dpart_v, dagg_ref.at[there], gsem.at[1]),
            ]
            backs[0].start()
            for j in range(tiles):
                dpart_v[:, cols(j)] = lax.dot_general(
                    dlin_v[chunk, :], weight[cols(j), :], (((1,), (1,)), ((), ())), preferred_element_type=F32
                ).astype(BF16)

            @pl.loop(0, clusters)
            def _(p):
                @pl.when(completed(p))
                def _():
                    @pl.when(p != first_completed)
                    def _():
                        start_all(load_back(p))

                    wait_all(load_back(p))
                    dagg_v[pl.ds(at(CHUNK + got_row - offset_of(p)), CHUNK), :] = dpart_v[...]
                    keep_live_rows(dagg_v, count_of(p))

                    def targets(j):
                        return [pltpu.make_async_copy(bnd_v.at[:, fine(j)], bnd_ref.at[slot_of(p), :, fine(j)], bndsem.at[0, j])]

                    boundary(back_ahat[...], targets)
                    for j in range(width // FINE):
                        wait_all(targets(j))

            backs[1].start()
            wait_all(backs)

        @pl.when(out_valid)
        def _():
            wait_all(outs)
            groups(lambda copy: copy.wait())

    def second():
        got_chunk = tick - 1
        got_row = start + got_chunk * CHUNK
        got_valid = (got_chunk >= 0) & (got_chunk < chunks)
        out_chunk = tick + 1 - lag
        out_row = start + out_chunk * CHUNK
        out_valid = (out_chunk >= 0) & (tick < chunks)

        def ends_in(p, row):
            return (end_of(p) > row) & (end_of(p) <= row + CHUNK)

        def splits(p, row):
            after = jnp.where(p + 1 < clusters, end_of(jnp.minimum(p + 1, clusters - 1)), row + 2 * CHUNK)
            return (count_of(p) > STEP) & ends_in(p, row) & (after > row + CHUNK)

        def fresh(p):
            return got_valid & ends_in(p, got_row)

        def begun(p):
            return (got_chunk > 0) & splits(p, got_row - CHUNK)

        def task(p):
            return fresh(p) | begun(p)

        def load(p):
            return [
                pltpu.make_async_copy(recv_ref.at[pl.ds(at(offset_of(p)), slots)], rows_in.at[body], xsem.at[0]),
                pltpu.make_async_copy(ahat_ref.at[slot_of(p)], back_ahat, asem.at[0]),
            ]

        def load_begun(p):
            return [
                pltpu.make_async_copy(agg_ref.at[pl.ds(at(offset_of(p) + STEP), slots - STEP)], agg_v.at[pl.ds(STEP, slots - STEP)], xsem.at[0]),
                pltpu.make_async_copy(ahat_ref.at[slot_of(p)], back_ahat, asem.at[0]),
                pltpu.make_async_copy(dagg_ref.at[pl.ds(at(offset_of(p)), STEP)], dagg_v.at[pl.ds(CHUNK, STEP)], asem.at[1]),
            ]

        def load_g(p, r):
            here = pl.ds(pl.multiple_of(r * STEP, STEP), STEP)
            return pltpu.make_async_copy(in_ref.at[slot_of(p), here], x_v.at[0, here], xsem.at[1])

        def first_step(p):
            return jnp.where(fresh(p), 0, 1)

        def last_step(p):
            split = fresh(p) & splits(p, got_row) & (tick < chunks)
            return jnp.where(split, 1, (count_of(p) + STEP - 1) // STEP)

        def start_loads(p):
            @pl.when(fresh(p))
            def _():
                start_all(load(p))

            @pl.when(jnp.logical_not(fresh(p)))
            def _():
                start_all(load_begun(p))

            @pl.loop(first_step(p), last_step(p))
            def _(r):
                load_g(p, r).start()

        load_got = pltpu.make_async_copy(got_ref.at[chunk], g_v, gsem.at[0])
        keep_got = pltpu.make_async_copy(got_ref.at[chunk], recv_ref.at[pl.ds(at(got_row), CHUNK)], gsem.at[1])
        put_next = pltpu.make_async_copy(send_ref.at[pl.ds(at(out_row), CHUNK)], next_ref, nextsem)
        first_task = first_of(task)
        some = first_task < clusters
        new = out_valid & some & (offset_of(jnp.minimum(first_task, clusters - 1)) < out_row + CHUNK)

        @pl.when(some)
        def _():
            start_loads(first_task)
            start_all([load_weight(j) for j in range(tiles)])

        @pl.when(got_valid)
        def _():
            load_got.start()

        @pl.when(out_valid & jnp.logical_not(new))
        def _():
            put_next.start()

        @pl.when(got_valid)
        def _():
            load_got.wait()

        @pl.loop(0, clusters)
        def _(p):
            @pl.when(task(p))
            def _():
                offset, count, slot = offset_of(p), count_of(p), slot_of(p)
                steps = (count + STEP - 1) // STEP
                is_fresh = fresh(p)
                partial = is_fresh & splits(p, got_row) & (tick < chunks)

                @pl.when(p != first_task)
                def _():
                    start_loads(p)

                def keep_agg(r):
                    here = pl.ds(pl.multiple_of(r * STEP, STEP), STEP)
                    return pltpu.make_async_copy(agg_v.at[here], agg_ref.at[pl.ds(at(offset + r * STEP), STEP)], outsem.at[0])

                @pl.when(is_fresh)
                def _():
                    wait_all(load(p))
                    rows_in[pl.ds(at(CHUNK + got_row - offset), CHUNK), :] = g_v[...]
                    keep_live_rows(rows_in, count)

                    @pl.loop(0, tiles)
                    def _(j):
                        agg_v[:, cols(j)] = jnp.dot(back_ahat[...], rows_in[body, cols(j)], preferred_element_type=F32).astype(BF16)

                    @pl.loop(0, steps)
                    def _(r):
                        keep_agg(r).start()

                @pl.when(jnp.logical_not(is_fresh))
                def _():
                    wait_all(load_begun(p))

                @pl.loop(first_step(p), last_step(p))
                def _(r):
                    load_g(p, r).wait()

                def outs(r):
                    here = pl.ds(pl.multiple_of(r * STEP, STEP), STEP)
                    there = pl.ds(at(offset + r * STEP), STEP)
                    return [
                        pltpu.make_async_copy(act_v.at[here], act_ref.at[slot, here], outsem.at[1]),
                        pltpu.make_async_copy(dlin_v.at[here], dlin_ref.at[there], outsem.at[2]),
                    ]

                @pl.loop(first_step(p), last_step(p))
                def _(r):
                    here = pl.ds(pl.multiple_of(r * STEP, STEP), STEP)
                    live = (lax.broadcasted_iota(jnp.int32, (STEP, 1), 0) + r * STEP < count).astype(F32)

                    @pl.loop(0, tiles)
                    def _(j):
                        @pl.when((p == first_task) & (r == first_step(p)))
                        def _():
                            load_weight(j).wait()

                        linear = jnp.dot(agg_v[here, :], weight[:, cols(j)], preferred_element_type=F32) + bias_ref[:, cols(j)].astype(F32)
                        value, factor = silu_of(linear, live)
                        act_v[here, cols(j)] = value.astype(BF16)
                        dlin_v[here, cols(j)] = (x_v[0, here, cols(j)].astype(F32) * factor).astype(BF16)

                    start_all(outs(r))

                    @pl.loop(0, tiles)
                    def _(j):
                        dagg_v[pl.ds(pl.multiple_of(CHUNK + r * STEP, CHUNK), STEP), cols(j)] = lax.dot_general(
                            dlin_v[here, :], weight[cols(j), :], (((1,), (1,)), ((), ())), preferred_element_type=F32
                        ).astype(BF16)

                keep_dagg = pltpu.make_async_copy(dagg_v.at[pl.ds(CHUNK, STEP)], dagg_ref.at[pl.ds(at(offset), STEP)], asem.at[1])

                @pl.when(partial)
                def _():
                    keep_dagg.start()
                    keep_dagg.wait()

                @pl.when(jnp.logical_not(partial))
                def _():
                    @pl.loop(steps, slots // STEP)
                    def _(r):
                        dagg_v[pl.ds(pl.multiple_of(CHUNK + r * STEP, CHUNK), STEP), :] = jnp.zeros((STEP, width), BF16)

                    def targets(j):
                        return [
                            pltpu.make_async_copy(bnd_v.at[:, fine(j)], send_ref.at[pl.ds(at(offset), slots), fine(j)], bndsem.at[0, j]),
                            pltpu.make_async_copy(bnd_v.at[:, fine(j)], bnd_ref.at[slot, :, fine(j)], bndsem.at[1, j]),
                        ]

                    boundary(back_ahat[...], targets)
                    for j in range(width // FINE):
                        wait_all(targets(j))

                @pl.loop(first_step(p), last_step(p))
                def _(r):
                    wait_all(outs(r))

                @pl.when(is_fresh)
                def _():
                    @pl.loop(0, steps)
                    def _(r):
                        keep_agg(r).wait()

        @pl.when(got_valid)
        def _():
            keep_got.start()

        @pl.when(new)
        def _():
            put_next.start()

        @pl.when(got_valid)
        def _():
            keep_got.wait()

        @pl.when(out_valid)
        def _():
            put_next.wait()

    pl.when(first_section)(first)
    pl.when(jnp.logical_not(first_section))(second)


def run_tick(tick, plan, section_rows, ahat, weight, bias, got, state, packed):
    clusters, slots, width = section_rows.shape
    tiles = width // TILE
    state_shapes = tuple(jax.ShapeDtypeStruct(s.shape, s.dtype) for s in state)
    cluster = pltpu.VMEM((slots, width), BF16)
    roomy = pltpu.VMEM((slots + 2 * CHUNK, width), BF16)
    chunk = pltpu.VMEM((CHUNK, width), BF16)
    chunk32 = pltpu.VMEM((CHUNK, width), F32)
    dma = pltpu.SemaphoreType.DMA
    outs = pl.pallas_call(
        functools.partial(tick_kernel, clusters, slots, width, packed),
        out_shape=(jax.ShapeDtypeStruct((CHUNK, width), BF16),) + state_shapes,
        in_specs=[SMEM, SMEM, ANY, ANY, ANY, VMEM, ANY] + [HBM] * 8,
        out_specs=(ANY,) + (HBM,) * 8,
        input_output_aliases={7 + i: 1 + i for i in range(8)},
        scratch_shapes=[
            pltpu.VMEM((width, width), BF16),
            pltpu.VMEM((2, slots + 2 * CHUNK, slots), BF16),
            pltpu.VMEM((slots, slots), BF16),
            roomy,
            pltpu.VMEM((2, slots, width), BF16),
            chunk, cluster, cluster, cluster, roomy, chunk, cluster, chunk32, chunk32,
            dma((tiles,)), dma((2,)), dma((2,)), dma((2,)), dma((2,)), dma((3,)), dma((2, width // FINE)), dma, dma,
        ],
        compiler_params=pltpu.CompilerParams(vmem_limit_bytes=57 << 20, has_side_effects=True),
        cost_estimate=pl.CostEstimate(flops=6 * CHUNK * width * width, bytes_accessed=2 * width * width, transcendentals=0),
    )(tick, plan, section_rows, ahat, weight, bias, got, *state)
    return outs[0], outs[1:]


def tracks_of(n, rows):
    weights = [2**q for q in range(n.bit_length() - 1)]
    part = rows // 4
    if len(weights) < 3 or part // n < 16:
        return [(0, rows, weights)]
    return [(0, rows - part, weights), (rows - part, part, [weights[0], weights[2], weights[1]] + weights[3:])]


def finish_kernel(
    n, block, halves, rows, back,
    agg_ref, dlin_ref, dfac_ref, send_ref, last_ref, weight_ref, out_ref, db_ref, dagg_ref,
    agg, dlin, acc, sbuf, rbuf, res, got, dfac, dsend, drecv, dsum, dacc, dagg_v, last_v,
    lsem, wsem, asem, dlsem, bsem, osem, ssem, rsem, gssem, grsem, dssem, drsem, xssem, xrsem,
):
    width = dlin.shape[1]
    slots, rows_out = acc.shape[0], acc.shape[1]
    nb = res.shape[0]
    column_blocks = nb // halves
    section = lax.axis_index("section")
    me = lax.axis_index("dp")
    tracks = tracks_of(n, rows_out)
    depth = len(tracks[0][2])
    late = pl.ds(rows - back, back)
    drained = pl.ds(rows - back + CHUNK, back - CHUNK)
    hops = [(s, m) for s in range(depth) for m in range(len(tracks))]

    def bit(m, s):
        return (me // tracks[m][2][s]) % 2

    def partner(s, m):
        return (section, me + (1 - 2 * bit(m, s)) * tracks[m][2][s])

    across = (1 - section, me)
    barrier = pltpu.get_barrier_semaphore()
    for s in range(depth):
        pl.semaphore_signal(barrier, inc=1, device_id=partner(s, 0), device_id_type=MESH)
    pl.semaphore_signal(barrier, inc=1, device_id=across, device_id_type=MESH)
    load_weight = pltpu.make_async_copy(weight_ref, agg, wsem)

    def load_agg(h):
        some = pl.ds(h * rows_out, rows_out)
        return pltpu.make_async_copy(agg_ref.at[pl.ds(0, rows), some], agg.at[:, some], asem.at[h])

    def load_dlin(c):
        some = pl.ds(pl.multiple_of(c * block, block), block)
        return pltpu.make_async_copy(dlin_ref.at[pl.ds(0, rows), some], dlin.at[:, some], dlsem.at[c])

    load_agg(0).start()
    load_dlin(0).start()
    for h in range(1, halves):
        load_agg(h).start()

    @pl.loop(1, column_blocks)
    def _(c):
        load_dlin(c).start()

    pl.semaphore_wait(barrier, depth + 1)

    def columns(c):
        return pl.ds(pl.multiple_of(c * block, block), block)

    def drain(c):
        return pltpu.make_async_remote_copy(
            src_ref=send_ref.at[drained, columns(c)], dst_ref=got.at[c], send_sem=xssem.at[c], recv_sem=xrsem.at[c],
            device_id=across, device_id_type=MESH)

    def load_back(c):
        return [
            pltpu.make_async_copy(dfac_ref.at[late, columns(c)], dfac.at[c % 2], bsem.at[c % 2, 0]),
            pltpu.make_async_copy(last_ref.at[:, columns(c)], last_v.at[c % 2], bsem.at[c % 2, 1]),
        ]

    @pl.when(section == 1)
    def _():
        for c in range(min(2, column_blocks)):
            drain(c).start()

    @pl.when(section == 0)
    def _():
        for copy in load_back(0):
            copy.start()

    def size(m, s):
        return tracks[m][1] >> s

    def piece(m, s):
        row = tracks[m][0]
        for q in range(s):
            row = row + bit(m, q) * size(m, q + 1)
        return row

    def other(m, s):
        return piece(m, s) + (1 - bit(m, s)) * size(m, s + 1)

    def rows_at(row, m, s):
        return pl.ds(pl.multiple_of(row, 16), size(m, s + 1))

    def staged(m, s):
        return pl.ds(tracks[m][0] + tracks[m][1] - size(m, s), size(m, s + 1))

    def rs(b, s, m):
        return pltpu.make_async_remote_copy(
            src_ref=sbuf.at[b, staged(m, s)], dst_ref=rbuf.at[b, staged(m, s)],
            send_sem=ssem.at[b, s, m], recv_sem=rsem.at[b, s, m], device_id=partner(s, m), device_id_type=MESH)

    def rs_start(b, s):
        for m in range(len(tracks)):
            sbuf[b, staged(m, s), :] = acc[b % slots, rows_at(other(m, s), m, s), :].astype(BF16)
            rs(b, s, m).start()

    def rs_end(b, s):
        for m in range(len(tracks)):
            here = rows_at(piece(m, s + 1), m, s)
            rs(b, s, m).wait_recv()
            total = acc[b % slots, here, :] + rbuf[b, staged(m, s), :].astype(F32)
            if s + 1 < depth:
                acc[b % slots, here, :] = total
            else:
                res[b, here, :] = total.astype(BF16)

    def ag(b, s, m, row):
        here = res.at[b, rows_at(row, m, s)]
        return pltpu.make_async_remote_copy(
            src_ref=here, dst_ref=here, send_sem=gssem.at[b, s, m], recv_sem=grsem.at[b, s, m],
            device_id=partner(s, m), device_id_type=MESH)

    def ag_start(b, s):
        for m in range(len(tracks)):
            ag(b, s, m, piece(m, s + 1)).start()

    def ag_end(b, s):
        for m in range(len(tracks)):
            ag(b, s, m, other(m, s)).wait_recv()

    def out(b):
        return pltpu.make_async_copy(res.at[b], out_ref.at[b], osem.at[b])

    def product(b):
        c = b // halves
        for h in range(halves):
            @pl.when(b == h)
            def _():
                load_agg(h).wait()

        @pl.when(b % halves == 0)
        def _():
            load_dlin(c).wait()

            @pl.when(section == 1)
            def _():
                drain(c).wait_send()

                @pl.when(c + 2 < column_blocks)
                def _():
                    drain(c + 2).start()

            @pl.when(section == 0)
            def _():
                for copy in load_back(c):
                    copy.wait()

                @pl.when(c + 1 < column_blocks)
                def _():
                    for copy in load_back(c + 1):
                        copy.start()

                last = last_v[c % 2]
                factor = dfac[c % 2, pl.ds(0, CHUNK)]
                value = jnp.where(factor == 0.0, 0.0, last.astype(F32) * factor)
                dlin[pl.ds(rows - back, CHUNK), columns(c)] = value.astype(BF16)
                drain(c).wait_recv()
                dlin[drained, columns(c)] = (got[c].astype(F32) * dfac[c % 2, pl.ds(CHUNK, back - CHUNK)]).astype(BF16)

            @pl.loop(0, rows // 256)
            def _(i):
                some = dlin[pl.ds(pl.multiple_of(i * 256, 256), 256), columns(c)].astype(F32)
                dacc[:, columns(c)] += jnp.sum(some.reshape(32, 8, block), axis=0)


        d = dlin[:, columns(c)]
        part = min(rows_out, 512 if slots < nb else 256)

        @pl.loop(0, rows_out // part)
        def _(i):
            r = pl.ds(pl.multiple_of(i * part, part), part)
            a = agg[:, pl.ds(pl.multiple_of((b % halves) * rows_out + i * part, part), part)]
            acc[b % slots, r, :] = lax.dot_general(a, d, (((0,), (0,)), ((), ())), preferred_element_type=F32)

    def stage(b, k):
        if k == 0:
            product(b)
            rs_start(b, 0)
        elif k < depth:
            rs_end(b, k - 1)
            rs_start(b, k)
        elif k == depth:
            rs_end(b, k - 1)
            ag_start(b, depth - 1)
        else:
            s = 2 * depth - k
            ag_end(b, s)
            if s > 0:
                ag_start(b, s - 1)
            else:
                out(b).start()

    bits = dsend.shape[0]

    def db(q):
        to = (section, me + (1 - 2 * ((me // 2**q) % 2)) * 2**q)
        return pltpu.make_async_remote_copy(
            src_ref=dsend.at[q], dst_ref=drecv.at[q], send_sem=dssem.at[q], recv_sem=drsem.at[q],
            device_id=to, device_id_type=MESH)

    def db_step(q):
        if q == 0:
            whole = jnp.sum(dacc[...], axis=0, keepdims=True)
            for i in range(8):
                dsum[i:i + 1, :] = whole[:, i * (width // 8):(i + 1) * (width // 8)]
        else:
            db(q - 1).wait_recv()
            dsum[...] += drecv[q - 1]
        if q < bits:
            dsend[q] = dsum[...]
            db(q).start()

    parts = back // dagg_v.shape[0]

    def dagg_part(i):
        size = dagg_v.shape[0]
        first = pl.multiple_of(rows - back + i * size, 32)

        @pl.loop(0, width // 512)
        def _(j):
            c = pl.ds(pl.multiple_of(j * 512, 512), 512)
            dagg_v[:, c] = lax.dot_general(
                dlin[pl.ds(first, size), :], agg[c, :], (((1,), (1,)), ((), ())), preferred_element_type=F32
            ).astype(BF16)

        copy = pltpu.make_async_copy(dagg_v, dagg_ref.at[pl.ds(pl.multiple_of(i * size, 32), size)], lsem.at[0])
        copy.start()
        copy.wait()

    dacc[...] = jnp.zeros_like(dacc)
    stages = 2 * depth + 1

    @pl.loop(0, nb + stages - 1)
    def _(step):
        for k in reversed(range(stages)):
            b = step - k

            @pl.when((b >= 0) & (b < nb))
            def _():
                stage(b, k)

        @pl.when((step == nb - 1) & (section == 0))
        def _():
            load_weight.start()

        for q in range(min(bits + 1, stages - 1)):
            @pl.when(step == nb + q)
            def _():
                db_step(q)

        @pl.when((step == nb) & (section == 0))
        def _():
            load_weight.wait()

        @pl.when((step >= nb) & (step < nb + parts) & (section == 0))
        def _():
            dagg_part(step - nb)

    for q in range(min(bits + 1, stages - 1), bits + 1):
        db_step(q)
    db_ref[...] = dsum[...]

    @pl.loop(0, nb)
    def _(b):
        for s, m in hops:
            rs(b, s, m).wait_send()
            ag(b, s, m, piece(m, s + 1)).wait_send()
        out(b).wait()

    for q in range(bits):
        db(q).wait_send()


def finish(n, agg, dlin, dfac, send, last, weight, rows, back):
    width = weight.shape[1]
    bits = n.bit_length() - 1
    block = 256
    halves = 2 if weight.shape[0] // n >= 128 else 1
    rows_out = weight.shape[0] // halves
    column_blocks = width // block
    nb = column_blocks * halves
    slots = min(nb, bits + 1)
    tracks = len(tracks_of(n, rows_out))
    dma = pltpu.SemaphoreType.DMA
    return pl.pallas_call(
        functools.partial(finish_kernel, n, block, halves, rows, back),
        out_shape=(
            jax.ShapeDtypeStruct((nb, rows_out, block), BF16),
            jax.ShapeDtypeStruct((8, width // 8), F32),
            jax.ShapeDtypeStruct((back, width), BF16),
        ),
        in_specs=[ANY] * 6,
        out_specs=(ANY, VMEM, ANY),
        scratch_shapes=[
            pltpu.VMEM((rows, weight.shape[0]), BF16),
            pltpu.VMEM((rows, width), BF16),
            pltpu.VMEM((slots, rows_out, block), F32),
            pltpu.VMEM((nb, rows_out, block), BF16),
            pltpu.VMEM((nb, rows_out, block), BF16),
            pltpu.VMEM((nb, rows_out, block), BF16),
            pltpu.VMEM((column_blocks, back - CHUNK, block), BF16),
            pltpu.VMEM((2, back, block), F32),
            pltpu.VMEM((bits, 8, width // 8), F32),
            pltpu.VMEM((bits, 8, width // 8), F32),
            pltpu.VMEM((8, width // 8), F32),
            pltpu.VMEM((8, width), F32),
            pltpu.VMEM((back // 4, width), BF16),
            pltpu.VMEM((2, CHUNK, block), BF16),
            dma((1,)), dma, dma((halves,)), dma((column_blocks,)), dma((2, 2)), dma((nb,)),
            dma((nb, bits, tracks)), dma((nb, bits, tracks)), dma((nb, bits, tracks)), dma((nb, bits, tracks)),
            dma((bits,)), dma((bits,)), dma((column_blocks,)), dma((column_blocks,)),
        ],
        compiler_params=pltpu.CompilerParams(collective_id=1, has_side_effects=True, vmem_limit_bytes=63 << 20),
        cost_estimate=pl.CostEstimate(flops=2 * rows * weight.shape[0] * width, bytes_accessed=rows * width * 8, transcendentals=0),
    )(agg, dlin, dfac, send, last, weight)


def closing_kernel(
    clusters, slots, packed, back, plan_ref, blocks_ref, sums_ref, ahat_ref, dagg_ref, late_ref, bnd_i,
    grad_ref, bias_ref, bnd_ref, ahat, source, bnd_v, sem, asem, osem,
):
    step = pl.program_id(0)
    first_section = lax.axis_index("section") == 0
    low = packed - back - slots
    loads = [
        pltpu.make_async_copy(dagg_ref.at[pl.ds(low, slots)], source.at[pl.ds(0, slots)], sem.at[0]),
        pltpu.make_async_copy(late_ref, source.at[pl.ds(slots, back)], sem.at[1]),
    ]

    def load_ahat(p):
        return pltpu.make_async_copy(ahat_ref.at[plan_ref[SLOT, p]], ahat.at[p], asem.at[p])

    def late(p):
        return first_section & (plan_ref[OFFSET, p] + plan_ref[COUNT, p] > packed - back)

    def store(p):
        return pltpu.make_async_copy(bnd_v.at[p % 2], bnd_ref.at[plan_ref[SLOT, p]], osem.at[p % 2])

    @pl.when(step == 0)
    def _():
        part = sums_ref.shape[1]
        for i in range(8):
            bias_ref[:, i * part:(i + 1) * part] = sums_ref[i:i + 1, :]

    @pl.when(first_section & (step == 0))
    def _():
        for load in loads:
            load.start()
        for p in range(clusters):
            @pl.when(late(p))
            def _():
                load_ahat(p).start()
        source[pl.ds(slots + back, slots), :] = jnp.zeros((slots, source.shape[1]), BF16)

    part = blocks_ref.shape[1]
    for i in range(blocks_ref.shape[0]):
        grad_ref[i * part:(i + 1) * part, :] = blocks_ref[i].astype(F32)

    @pl.when(first_section & (step == 2))
    def _():
        for load in loads:
            load.wait()

    half = source.shape[1] // 2
    for p in reversed(range(clusters)):
        begin = 2 + 2 * (clusters - 1 - p)

        @pl.when((step == begin) & late(p))
        def _():
            load_ahat(p).wait()

        if p + 2 < clusters:
            @pl.when((step == begin) & late(p + 2))
            def _():
                store(p + 2).wait()

        @pl.when(((step == begin) | (step == begin + 1)) & late(p))
        def _():
            rows = pl.ds(pl.multiple_of(plan_ref[OFFSET, p] - low, GROUP), slots)
            cols = pl.ds(pl.multiple_of((step - begin) * half, half), half)
            bnd_v[p % 2, :, cols] = lax.dot_general(
                ahat[p], source[rows, cols], (((0,), (0,)), ((), ())), preferred_element_type=F32
            ).astype(BF16)

        @pl.when((step == begin + 1) & late(p))
        def _():
            store(p).start()

    for p in range(min(2, clusters)):
        @pl.when((step == pl.num_programs(0) - 1) & late(p))
        def _():
            store(p).wait()


def closing(plan, blocks, sums, ahat, dagg, late, bnd, packed):
    nb, rows, block = blocks.shape
    clusters, slots, width = bnd.shape
    halves = nb * block // width
    column_blocks = nb // halves
    back = late.shape[0]
    steps = max(column_blocks, 2 * clusters + 2)
    return pl.pallas_call(
        functools.partial(closing_kernel, clusters, slots, packed, back),
        grid=(steps,),
        out_shape=(
            jax.ShapeDtypeStruct((rows * halves, width), F32),
            jax.ShapeDtypeStruct((1, width), F32),
            jax.ShapeDtypeStruct(bnd.shape, BF16),
        ),
        in_specs=[SMEM, pl.BlockSpec((halves, rows, block), lambda b: (jnp.minimum(b, column_blocks - 1), 0, 0)), VMEM] + [ANY] * 4,
        out_specs=(
            pl.BlockSpec((rows * halves, block), lambda b: (0, jnp.minimum(b, column_blocks - 1))),
            pl.BlockSpec((1, width), lambda b: (0, 0)),
            ANY,
        ),
        input_output_aliases={6: 2},
        scratch_shapes=[
            pltpu.VMEM((clusters, slots, slots), BF16),
            pltpu.VMEM((2 * slots + back, width), BF16),
            pltpu.VMEM((2, slots, width), BF16),
            pltpu.SemaphoreType.DMA((2,)),
            pltpu.SemaphoreType.DMA((clusters,)),
            pltpu.SemaphoreType.DMA((2,)),
        ],
        compiler_params=pltpu.CompilerParams(vmem_limit_bytes=60 << 20, has_side_effects=True),
    )(plan, blocks, sums, ahat, dagg, late, bnd)


def per_device(section_inputs, neighbours, counts, weight, bias):
    section_rows = section_inputs[0]
    weight_one = weight[0]
    clusters, slots, width = section_rows.shape
    packed = clusters * slots
    back = lag_of(slots) * CHUNK
    ahat, plan, *state = prepare(counts, jnp.swapaxes(neighbours, 1, 2), width, packed, slots)
    state = tuple(state)
    swap = [(0, 1), (1, 0)]

    def step(tick, got, state):
        return run_tick(tick, plan, section_rows, ahat, weight_one, bias, got, state, packed)

    first = jnp.full((1,), -1, jnp.int32)
    send, state = step(first, weight_one, state)
    send, last_plan = lax.optimization_barrier((send, plan))
    chunks = last_plan[REST, CHUNKS]

    def more(carry):
        return carry[0][0] <= chunks

    def body(carry):
        tick, send, got, state = carry
        arrives = lax.ppermute(send, "section", swap)
        send, state = step(tick, got, state)
        return tick + 1, send, arrives, state

    tick, send, got, state = lax.while_loop(more, body, (first + 1, send, send, state))
    agg, dlin, dfac, to_send, recv, dagg, act, bnd = state
    blocks, sums, late = finish(lax.axis_size("dp"), agg, dlin, dfac, to_send, got, weight_one, packed, back)
    grad_weight, grad_bias, bnd = closing(plan, blocks, sums, ahat, dagg, late, bnd, packed)
    return act[None], bnd[None], grad_weight[None], grad_bias


def solution(mesh):
    return jax.shard_map(
        per_device,
        mesh=mesh,
        in_specs=(
            P("section", "dp", None, None),
            P("dp", None, None),
            P("dp"),
            P("section", None, None),
            P("section", None),
        ),
        out_specs=(
            P("section", "dp", None, None),
            P("section", "dp", None, None),
            P("section", None, None),
            P("section", None),
        ),
        check_vma=False,
    )
```
